512 devices in a mesh: dp: 8 (over x, z_hi), fsdp: 64 (over y, z_lo, core).
Axes of the slice: x: 4, y: 4, z: 16 (z_hi: 2, z_lo: 8; z = z_hi * 8 + z_lo), core: 2. Of those that a mesh axis runs over, the one named last changes fastest.
Arguments:
- tokens: bfloat16 [65536, 3584], P(('dp', 'fsdp')), may hold values from -6 to 6
- out_grad: bfloat16 [65536, 14336], P(('dp', 'fsdp')), may hold values from -6 to 6
- block_values: bfloat16 [320, 128, 128], P('fsdp'), may hold values from -0.3125 to 0.3125
- active_blocks: int32 [320, 2], P('fsdp'), may hold values from 0 to 111, as said below
- drop_slots: int32 [64], P('fsdp'), may hold values from 0 to 4, as said below
- cand_blocks: int32 [64, 2], replicated, may hold values from 0 to 111, as said below
- group_counts: int32 [8], P('dp'), may hold values from 4096 to 8192
Outputs:
- cand_grad: float32 [64, 128, 128], P('fsdp')
- cand_score: float32 [64], P('fsdp')
The draws below stay inside these ranges and needn't reach their ends.
Inputs may be any that keep to these rules, and one draw needn't show every extreme that they name: `active_blocks`: pairs of block row (below D / 128) and block column (below 14336 / 128); all pairs distinct. `drop_slots`: the 1 entries of each device are distinct local slots. `cand_blocks`: pairs of block row and block column, distinct, none of them a stored block.
All inputs are finite; a program needn't handle non-finite values.
Results may differ from the reference program's by a relative error of at most 0.007.
Values may be sent and summed in bfloat16 or wider, within the bound.
No kernel may reach another device: no remote copies, remote signals or barrier semaphores. Data moves between devices by JAX's collectives and lax.ppermute only.
A program may use at most 128 MiB of HBM per device.

```python
import math
import jax
import jax.numpy as jnp
from jax import lax

D = 3584
FF = 14336
BLK = 128
TOK_DEV = 128
K_DEV = 5
DROP_DEV = 1
GROUP_TOK = 8192
TOKENS = 65536
K = 320
DROPS = 64
CANDS = 64
N_DP = 8
N_FSDP = 64


def block_order(key):
    return jax.random.permutation(key, D // BLK * (FF // BLK)).astype(jnp.int32)


def draw_active_blocks(key, part):
    shared = block_order(key)[:K]
    return jnp.stack([shared // (FF // BLK), shared % (FF // BLK)], axis=1).astype(jnp.int32)


def draw_cand_blocks(key, part):
    shared = block_order(key)[K:K + CANDS]
    return jnp.stack([shared // (FF // BLK), shared % (FF // BLK)], axis=1).astype(jnp.int32)


def draw_drop_slots(key, part):
    key = jax.random.fold_in(key, 3)
    subkeys = jax.random.split(key, K // K_DEV)
    picked = jax.vmap(lambda single: jax.random.permutation(single, K_DEV)[:DROP_DEV])(subkeys)
    return picked.reshape(-1).astype(jnp.int32)


def set_ends(drawn, rng, least, largest):
    longest = drawn.shape.index(max(drawn.shape))
    spots = []
    for shift in (0, 1):
        where = [jax.random.randint(jax.random.fold_in(rng, axis), (), 0, length) for axis, length in enumerate(drawn.shape)]
        where[longest] = (where[longest] + shift) % drawn.shape[longest]
        spots.append(tuple(where))
    return drawn.at[spots[0]].set(least).at[spots[1]].set(largest)


def level_of(rng, shape, pieces, least, largest):
    def one(axis_at, blocks):
        heights = jax.random.uniform(jax.random.fold_in(jax.random.fold_in(rng, 6), axis_at), (blocks,), jnp.float32, least / len(pieces), largest / len(pieces))
        return jnp.repeat(jnp.exp(heights), shape[axis_at] // blocks).reshape((-1,) + (1,) * (len(shape) - axis_at - 1))

    loudness = one(*pieces[0])
    for cut in pieces[1:]:
        loudness = loudness * one(*cut)
    return loudness


def centred(rng, extent, width, reach, cuts=(), kind=jnp.bfloat16):
    factor_of = level_of(rng, extent, cuts, -0.22, 0.18) if cuts else 1.0
    values = jax.random.normal(rng, extent, jnp.float32) * width * factor_of
    return jnp.minimum(jnp.maximum(values, -reach), reach).astype(kind)


def setup_inputs(seed: int = 0) -> dict:
    keys = jax.random.split(jax.random.key(seed), 8)
    tokens = centred(keys[0], (TOKENS, D), 1.0, 6.0, ((0, 512),))
    out_grad = centred(keys[1], (TOKENS, FF), 1.0, 6.0, ((0, 512),))
    block_values = centred(keys[2], (K, BLK, BLK), (K * BLK * BLK // FF) ** -0.5, 0.3125, ((0, 64),))
    active_blocks = draw_active_blocks(jax.random.fold_in(keys[7], 71), 0)
    drop_slots = draw_drop_slots(jax.random.fold_in(keys[7], 71), 0)
    cand_blocks = draw_cand_blocks(jax.random.fold_in(keys[7], 71), 0)
    group_counts = set_ends(jax.random.randint(keys[6], (N_DP,), GROUP_TOK // 2, GROUP_TOK + 1), jax.random.fold_in(keys[6], 1), GROUP_TOK // 2, GROUP_TOK).astype(jnp.int32)
    return dict(tokens=tokens, out_grad=out_grad, block_values=block_values, active_blocks=active_blocks, drop_slots=drop_slots, cand_blocks=cand_blocks, group_counts=group_counts)


def gelu_slope(value_in):
    normal_cdf = 0.5 * (1.0 + jax.scipy.special.erf(value_in * 0.7071067811865476))
    density = jnp.exp(-0.5 * value_in * value_in) * 0.3989422804014327
    return normal_cdf + value_in * density

def reference(tokens, out_grad, block_values, active_blocks, drop_slots, cand_blocks, group_counts):
    row_blocks = D // BLK
    col_blocks = FF // BLK
    owners = jnp.arange(DROPS, dtype=jnp.int32) // DROP_DEV
    kept_flag = jnp.ones((K,), jnp.float32).at[owners * K_DEV + drop_slots].set(0.0)
    weights = block_values.astype(jnp.float32) * kept_flag[:, None, None]
    block_rows = active_blocks[:, 0]
    block_cols = active_blocks[:, 1]
    cand_rows = cand_blocks[:, 0]
    cand_cols = cand_blocks[:, 1]
    devices_all = N_DP * N_FSDP
    tok_split = tokens.reshape(devices_all, TOK_DEV, row_blocks, BLK)
    grad_split = out_grad.reshape(devices_all, TOK_DEV, FF)

    def advance(summed, sliced):
        device_id, tok_block, grad_block = sliced
        picked = tok_block[:, block_rows, :].astype(jnp.float32)
        product = jnp.einsum('tkb,kbc->tkc', picked, weights)
        preact = jnp.zeros((TOK_DEV, col_blocks, BLK), jnp.float32).at[:, block_cols, :].add(product)
        preact = preact.reshape(TOK_DEV, FF)
        group_id = device_id // N_FSDP
        position = device_id % N_FSDP * TOK_DEV + jnp.arange(TOK_DEV, dtype=jnp.int32)
        usable = (position < group_counts[group_id]).astype(jnp.float32)
        pre_grad = (grad_block.astype(jnp.float32) * gelu_slope(preact) * usable[:, None]).astype(jnp.bfloat16)
        cand_x = tok_block[:, cand_rows, :].astype(jnp.float32)
        cand_dy = pre_grad.reshape(TOK_DEV, col_blocks, BLK)[:, cand_cols, :].astype(jnp.float32)
        return (summed + jnp.einsum('tcb,tce->cbe', cand_x, cand_dy), None)
    summed, _ = lax.scan(advance, jnp.zeros((CANDS, BLK, BLK), jnp.float32), (jnp.arange(devices_all, dtype=jnp.int32), tok_split, grad_split))
    cand_grad = summed * (1.0 / math.sqrt(TOKENS))
    cand_score = jnp.sqrt(lax.optimization_barrier(jnp.mean(cand_grad * cand_grad, axis=(1, 2))) + 1e-06)
    return (cand_grad, cand_score)
```

```python
import functools

import jax
import jax.numpy as jnp
from jax import lax
from jax.experimental import pallas as pl
from jax.experimental.pallas import tpu as pltpu
from jax.sharding import Mesh, PartitionSpec as P

AXES = ("x", "zh", "y", "zl", "c")
SIZES = (4, 2, 4, 8, 2)
NX, NZH, NY, NZL, NC = SIZES
BLK = 128
TAIL = 16
PIECE = NZL * BLK + TAIL


def lines(axis_of_core):
    def flat(x, zh, y, zl, c):
        return (((x * NZH + zh) * NY + y) * NZL + zl) * NC + c

    groups = []
    for c, axis in enumerate(axis_of_core):
        for zh in range(NZH):
            for zl in range(NZL):
                for other in range(4):
                    if axis == "y":
                        groups.append([flat(other, zh, y, zl, c) for y in range(NY)])
                    else:
                        groups.append([flat(x, zh, other, zl, c) for x in range(NX)])
    return groups


def to_all(value, axis, count, groups=None):
    copies = jnp.broadcast_to(value[None], (count,) + value.shape)
    return lax.all_to_all(copies, axis, 0, 0, axis_index_groups=groups, tiled=True)


def gelu_slope(value_in):
    normal_cdf = 0.5 * (1.0 + lax.erf(value_in * 0.7071067811865476))
    density = jnp.exp(-0.5 * value_in * value_in) * 0.3989422804014327
    return normal_cdf + value_in * density


def local_kernel(
    stored, places, cand, info,
    tok_ref, grad_hbm, own_hbm, other_hbm,
    out_ref,
    weights, grad, acc, pre, need, rows, cols, offs, used, sems,
):
    half = own_hbm.shape[0]
    copy_own = pltpu.make_async_copy(own_hbm, weights.at[pl.ds(0, half)], sems.at[0])
    copy_other = pltpu.make_async_copy(other_hbm, weights.at[pl.ds(half, half)], sems.at[1])
    copy_grad = pltpu.make_async_copy(grad_hbm, grad, sems.at[2])
    copy_own.start()
    copy_other.start()
    copy_grad.start()
    spare = acc.shape[0] - 1
    cands = cand.shape[0] // 2
    tokens = tok_ref.shape[0]

    def clear(i, carry):
        need[i] = 0
        return carry

    lax.fori_loop(0, spare + 1, clear, 0, unroll=8)

    def mark(j, count):
        col = cand[2 * j + 1]
        fresh = 1 - need[col]
        need[col] = 1
        used[count] = col
        acc[col] = jnp.zeros((tokens, BLK), jnp.float32)
        return count + fresh

    n_cols = lax.fori_loop(0, cands, mark, 0, unroll=4)

    def choose(k, count):
        col = places[2 * k + 1]
        rows[count] = places[2 * k]
        cols[count] = col
        offs[count] = (k // NZL) * PIECE + (k % NZL) * BLK
        return count + need[col]

    n_blocks = lax.fori_loop(0, stored, choose, 0, unroll=8)
    for u in range(4):
        rows[n_blocks + u] = 0
        cols[n_blocks + u] = spare
        offs[n_blocks + u] = 0
    copy_own.wait()
    copy_other.wait()

    def multiply(step, carry):
        products = []
        for u in range(4):
            i = step * 4 + u
            row = pl.multiple_of(rows[i] * BLK, BLK)
            off = pl.multiple_of(offs[i], 16)
            products.append(
                jnp.dot(
                    tok_ref[:, pl.ds(row, BLK)],
                    weights[pl.ds(off, BLK), :],
                    preferred_element_type=jnp.float32,
                )
            )
        for u in range(4):
            i = step * 4 + u
            acc[cols[i]] += products[u]
        return carry

    lax.fori_loop(0, (n_blocks + 3) // 4, multiply, 0)
    copy_grad.wait()
    position = info[0] + lax.broadcasted_iota(jnp.int32, (tokens, BLK), 0)
    usable = (position < info[1]).astype(jnp.float32)

    def slope(i, carry):
        col = used[i]
        lanes = pl.ds(pl.multiple_of(col * BLK, BLK), BLK)
        given = grad[:, lanes].astype(jnp.float32)
        pre[col] = (given * gelu_slope(acc[col]) * usable).astype(jnp.bfloat16)
        return carry

    lax.fori_loop(0, n_cols, slope, 0)

    def gradient(q, carry):
        y, z = q // NZL, q % NZL
        for core in range(NC):
            j = q * NC + core
            row = pl.multiple_of(cand[2 * j] * BLK, BLK)
            part = lax.dot_general(
                tok_ref[:, pl.ds(row, BLK)],
                pre[cand[2 * j + 1]],
                (((0,), (0,)), ((), ())),
                preferred_element_type=jnp.float32,
            ).astype(jnp.bfloat16)
            for x in range(NX):
                out_ref[core, x, y, z] = part[x * 32 : (x + 1) * 32]
        return carry

    lax.fori_loop(0, cands // NC, gradient, 0, unroll=2)


def local_part(tokens, out_grad, own, other, places, cand, info):
    stored = places.shape[0] // 2
    col_blocks = out_grad.shape[1] // BLK
    rows_dev = tokens.shape[0]
    shape = (NC, NX, NY, NZL, BLK // NX, BLK)
    smem = lambda count: pltpu.SMEM((count,), jnp.int32)
    return pl.pallas_call(
        functools.partial(local_kernel, stored),
        out_shape=jax.ShapeDtypeStruct(shape, jnp.bfloat16),
        grid_spec=pltpu.PrefetchScalarGridSpec(
            num_scalar_prefetch=3,
            grid=(),
            in_specs=[
                pl.BlockSpec(memory_space=pltpu.VMEM),
                pl.BlockSpec(memory_space=pl.ANY),
                pl.BlockSpec(memory_space=pl.ANY),
                pl.BlockSpec(memory_space=pl.ANY),
            ],
            out_specs=pl.BlockSpec(memory_space=pltpu.VMEM),
            scratch_shapes=[
                pltpu.VMEM((2 * own.shape[0], BLK), jnp.bfloat16),
                pltpu.VMEM(out_grad.shape, jnp.bfloat16),
                pltpu.VMEM((col_blocks + 1, rows_dev, BLK), jnp.float32),
                pltpu.VMEM((col_blocks, rows_dev, BLK), jnp.bfloat16),
                smem(col_blocks + 1),
                smem(stored + 8),
                smem(stored + 8),
                smem(stored + 8),
                smem(cand.shape[0] // 2 + 8),
                pltpu.SemaphoreType.DMA((3,)),
            ],
        ),
        compiler_params=pltpu.CompilerParams(vmem_limit_bytes=48 * 1024 * 1024),
        cost_estimate=pl.CostEstimate(
            flops=2 * (stored + 64) * rows_dev * BLK * BLK,
            bytes_accessed=20_000_000,
            transcendentals=2_000_000,
        ),
    )(places, cand, info, tokens, out_grad, own, other)


def per_device(
    tokens, out_grad, block_values, active_blocks, drop_slots, cand_blocks, group_counts
):
    rows_dev = tokens.shape[0]
    me = {name: lax.axis_index(name) for name in AXES}
    slot = me["x"] + (me["x"] >= drop_slots[0]).astype(jnp.int32)
    block = lax.dynamic_index_in_dim(block_values, slot, 0, keepdims=False)
    place = lax.dynamic_index_in_dim(active_blocks, slot, 0, keepdims=False)
    lane = lax.broadcasted_iota(jnp.int32, (TAIL, BLK), 1)
    tail = jnp.where(lane == 0, place[0], jnp.where(lane == 1, place[1], 0))
    piece = jnp.concatenate([block, tail.astype(jnp.bfloat16)], axis=0)
    along_z = to_all(piece, "zl", NZL).reshape(NZL, BLK + TAIL, BLK)
    tails = jnp.pad(along_z[:, BLK, :], ((0, TAIL - NZL), (0, 0)))
    pack = jnp.concatenate([along_z[:, :BLK, :].reshape(NZL * BLK, BLK), tails], axis=0)
    line = to_all(pack, AXES, 4, lines("yx"))
    plane = to_all(line.reshape(4 * PIECE, BLK), AXES, 4, lines("xy")).reshape(16 * PIECE, BLK)
    other = lax.ppermute(plane, "c", [(0, 1), (1, 0)])

    def places_of(part):
        return part.reshape(16, PIECE, BLK)[:, NZL * BLK : NZL * BLK + NZL, :2]

    places = jnp.stack([places_of(plane), places_of(other)]).astype(jnp.int32).reshape(-1)
    fsdp = (me["y"] * NZL + me["zl"]) * NC + me["c"]
    info = jnp.stack([fsdp * rows_dev, group_counts[0]]).astype(jnp.int32)
    partial = local_part(
        tokens, out_grad, plane, other, places, cand_blocks.reshape(-1), info
    )
    pair = lax.all_to_all(partial, "c", 0, 0, tiled=True)
    mine = jnp.sum(pair.astype(jnp.float32), axis=0).astype(jnp.bfloat16)
    mine = mine.reshape(NX * NY, NZL, BLK // NX, BLK)
    planes = lax.all_to_all(mine, ("x", "y"), 0, 0, tiled=True)
    strip = jnp.sum(planes.astype(jnp.float32), axis=0).astype(jnp.bfloat16)
    strips = jnp.broadcast_to(strip[None], (NZH,) + strip.shape).reshape(NZH * NZL, BLK // NX, BLK)
    strips = lax.all_to_all(strips, ("zh", "zl"), 0, 0, tiled=True)
    summed = jnp.sum(strips.astype(jnp.float32), axis=0)
    whole = to_all(summed, "x", NX).reshape(1, BLK, BLK)
    scale = (rows_dev * NX * NZH * NY * NZL * NC) ** (-0.5)
    cand_grad = whole * scale
    cand_score = jnp.sqrt(jnp.mean(cand_grad * cand_grad, axis=(1, 2)) + 1e-06)
    return (cand_grad, cand_score)


def solution(mesh):
    fine = Mesh(mesh.devices.reshape(SIZES), AXES)
    dp, fsdp = ("x", "zh"), ("y", "zl", "c")
    return jax.shard_map(
        per_device,
        mesh=fine,
        in_specs=(
            P(AXES, None),
            P(AXES, None),
            P(fsdp, None, None),
            P(fsdp, None),
            P(fsdp),
            P(),
            P(dp),
        ),
        out_specs=(P(fsdp, None, None), P(fsdp)),
        check_vma=False,
    )
```

```python
import jax
import jax.numpy as jnp
from jax import lax
from jax.experimental import pallas as pl
from jax.experimental.pallas import tpu as pltpu
from jax.sharding import Mesh, PartitionSpec as P

AXES = ("x", "zh", "y", "zl", "c")
SIZES = (4, 2, 4, 8, 2)
NX, NZH, NY, NZL, NC = SIZES
BLK = 128
TAIL = 16
PIECE = NZL * BLK + TAIL
MUL = 8


def flat(x, zh, y, zl, c):
    return (((x * NZH + zh) * NY + y) * NZL + zl) * NC + c


def runs_along_z():
    return [
        [flat(x, (z // NZL) % NZH, y, z % NZL, c) for z in range(start, start + NZL)]
        for c in range(NC)
        for x in range(NX)
        for y in range(NY)
        for start in (4 * c, 4 * c + NZL)
    ]


def lines(axis_of_core):
    groups = []
    for c, axis in enumerate(axis_of_core):
        for zh in range(NZH):
            for zl in range(NZL):
                for other in range(4):
                    if axis == "y":
                        groups.append([flat(other, zh, y, zl, c) for y in range(NY)])
                    else:
                        groups.append([flat(x, zh, other, zl, c) for x in range(NX)])
    return groups


def to_all(value, axis, count, groups=None):
    copies = jnp.broadcast_to(value[None], (count,) + value.shape)
    return lax.all_to_all(copies, axis, 0, 0, axis_index_groups=groups, tiled=True)


def gelu_slope(value_in):
    normal_cdf = 0.5 * (1.0 + lax.erf(value_in * 0.7071067811865476))
    density = jnp.exp(-0.5 * value_in * value_in) * 0.3989422804014327
    return normal_cdf + value_in * density


def choose_blocks(places, slot_of, rows, slots, offs, spare, unroll):
    def choose(k, count):
        slot = slot_of[places[2 * k + 1]]
        rows[count] = places[2 * k]
        slots[count] = slot
        offs[count] = (k // NZL) * PIECE + (k % NZL) * BLK
        return count + (slot != spare).astype(jnp.int32)

    count = lax.fori_loop(0, places.shape[0] // 2, choose, 0, unroll=8)
    for u in range(unroll):
        rows[count + u] = 0
        slots[count + u] = spare
        offs[count + u] = 0
    return count


def give_slots(cand, slot_of, used, spare):
    def clear(i, carry):
        slot_of[i] = spare
        return carry

    lax.fori_loop(0, slot_of.shape[0], clear, 0, unroll=8)

    def mark(j, count):
        col = cand[2 * j + 1]
        had = slot_of[col]
        fresh = had == spare
        slot_of[col] = jnp.where(fresh, count, had)
        used[count] = col
        return count + fresh.astype(jnp.int32)

    return lax.fori_loop(0, cand.shape[0] // 2, mark, 0, unroll=4)


def add_products(count, tok_ref, weights, acc, rows, slots, offs, unroll):
    def multiply(step, carry):
        products = []
        for u in range(unroll):
            i = step * unroll + u
            row = pl.multiple_of(rows[i] * BLK, BLK)
            off = pl.multiple_of(offs[i], 16)
            products.append(
                jnp.dot(
                    tok_ref[:, pl.ds(row, BLK)],
                    weights[pl.ds(off, BLK), :],
                    preferred_element_type=jnp.float32,
                )
            )
        for u in range(unroll):
            acc[slots[step * unroll + u]] += products[u]
        return carry

    lax.fori_loop(0, (count + unroll - 1) // unroll, multiply, 0)


def first_kernel(
    places, cand, tok_ref, own_hbm, acc,
    weights, slot_of, used, rows, slots, offs, sem,
):
    copy_own = pltpu.make_async_copy(own_hbm, weights, sem.at[0])
    copy_own.start()
    spare = acc.shape[0] - 1
    give_slots(cand, slot_of, used, spare)

    def zero(i, carry):
        acc[i] = jnp.zeros(acc.shape[1:], jnp.float32)
        return carry

    lax.fori_loop(0, spare + 1, zero, 0, unroll=5)
    count = choose_blocks(places, slot_of, rows, slots, offs, spare, MUL)
    copy_own.wait()
    add_products(count, tok_ref, weights, acc, rows, slots, offs, MUL)


def second_kernel(
    places, cand, info, tok_ref, grad_hbm, other_hbm, first, out_ref,
    weights, grad, acc, pre, slot_of, used, rows, slots, offs, sem,
):
    copy_other = pltpu.make_async_copy(other_hbm, weights, sem.at[0])
    copy_grad = pltpu.make_async_copy(grad_hbm, grad, sem.at[1])
    copy_other.start()
    copy_grad.start()
    spare = acc.shape[0] - 1
    tokens = tok_ref.shape[0]
    n_cols = give_slots(cand, slot_of, used, spare)

    def zero(i, carry):
        acc[i] = jnp.zeros(acc.shape[1:], jnp.float32)
        return carry

    lax.fori_loop(0, spare + 1, zero, 0, unroll=5)
    count = choose_blocks(places, slot_of, rows, slots, offs, spare, MUL)
    copy_other.wait()
    add_products(count, tok_ref, weights, acc, rows, slots, offs, MUL)
    copy_grad.wait()
    position = info[0] + lax.broadcasted_iota(jnp.int32, (tokens, BLK), 0)
    usable = (position < info[1]).astype(jnp.float32)

    def slope(i, carry):
        lanes = pl.ds(pl.multiple_of(used[i] * BLK, BLK), BLK)
        given = grad[:, lanes].astype(jnp.float32)
        preact = first[i] + acc[i]
        pre[i] = (given * gelu_slope(preact) * usable).astype(jnp.bfloat16)
        return carry

    lax.fori_loop(0, n_cols, slope, 0)

    def gradient(q, carry):
        y, z = q // NZL, q % NZL
        for core in range(NC):
            j = q * NC + core
            row = pl.multiple_of(cand[2 * j] * BLK, BLK)
            part = lax.dot_general(
                tok_ref[:, pl.ds(row, BLK)],
                pre[slot_of[cand[2 * j + 1]]],
                (((0,), (0,)), ((), ())),
                preferred_element_type=jnp.float32,
            ).astype(jnp.bfloat16)
            for x in range(NX):
                out_ref[core, x, y, z] = part[x * 32 : (x + 1) * 32]
        return carry

    lax.fori_loop(0, cand.shape[0] // (2 * NC), gradient, 0, unroll=4)


def lists(cols, cands, stored):
    smem = lambda count: pltpu.SMEM((count,), jnp.int32)
    return [smem(cols), smem(cands + 8)] + [smem(stored + 2 * MUL)] * 3


VMEM = pl.BlockSpec(memory_space=pltpu.VMEM)
ANY = pl.BlockSpec(memory_space=pl.ANY)


def first_half(tokens, own, places, cand, col_blocks):
    stored, cands = places.shape[0] // 2, cand.shape[0] // 2
    rows_dev = tokens.shape[0]
    return pl.pallas_call(
        first_kernel,
        out_shape=jax.ShapeDtypeStruct((cands + 1, rows_dev, BLK), jnp.float32),
        grid_spec=pltpu.PrefetchScalarGridSpec(
            num_scalar_prefetch=2,
            grid=(),
            in_specs=[VMEM, ANY],
            out_specs=VMEM,
            scratch_shapes=[pltpu.VMEM(own.shape, jnp.bfloat16)]
            + lists(col_blocks, cands, stored)
            + [pltpu.SemaphoreType.DMA((1,))],
        ),
        compiler_params=pltpu.CompilerParams(vmem_limit_bytes=20 * 1024 * 1024),
        cost_estimate=pl.CostEstimate(
            flops=2 * stored * rows_dev * BLK * BLK, bytes_accessed=10_000_000, transcendentals=0
        ),
    )(places, cand, tokens, own)


def second_half(tokens, out_grad, other, first, places, cand, info):
    stored, cands = places.shape[0] // 2, cand.shape[0] // 2
    col_blocks = out_grad.shape[1] // BLK
    rows_dev = tokens.shape[0]
    return pl.pallas_call(
        second_kernel,
        out_shape=jax.ShapeDtypeStruct((NC, NX, NY, NZL, BLK // NX, BLK), jnp.bfloat16),
        grid_spec=pltpu.PrefetchScalarGridSpec(
            num_scalar_prefetch=3,
            grid=(),
            in_specs=[VMEM, ANY, ANY, VMEM],
            out_specs=VMEM,
            scratch_shapes=[
                pltpu.VMEM(other.shape, jnp.bfloat16),
                pltpu.VMEM(out_grad.shape, jnp.bfloat16),
                pltpu.VMEM((cands + 1, rows_dev, BLK), jnp.float32),
                pltpu.VMEM((cands, rows_dev, BLK), jnp.bfloat16),
            ]
            + lists(col_blocks, cands, stored)
            + [pltpu.SemaphoreType.DMA((2,))],
        ),
        compiler_params=pltpu.CompilerParams(vmem_limit_bytes=32 * 1024 * 1024),
        cost_estimate=pl.CostEstimate(
            flops=2 * (stored + cands) * rows_dev * BLK * BLK,
            bytes_accessed=15_000_000,
            transcendentals=2_000_000,
        ),
    )(places, cand, info, tokens, out_grad, other, first)


def per_device(
    tokens, out_grad, block_values, active_blocks, drop_slots, cand_blocks, group_counts
):
    rows_dev = tokens.shape[0]
    me = {name: lax.axis_index(name) for name in AXES}
    slots = lax.broadcasted_iota(jnp.int32, (block_values.shape[0],), 0)
    mine = slots == me["x"] + (me["x"] >= drop_slots).astype(jnp.int32)
    block = jnp.sum(jnp.where(mine[:, None, None], block_values, 0), axis=0)
    place = jnp.sum(jnp.where(mine[:, None], active_blocks, 0), axis=0)
    tail = jnp.pad(place.astype(jnp.bfloat16)[None, :], ((0, 7), (0, BLK - 2)))
    piece = jnp.concatenate([block, tail], axis=0)
    along_z = to_all(piece, AXES, NZL, runs_along_z())
    tails = jnp.pad(along_z[:, BLK, :], ((0, TAIL - NZL), (0, 0)))
    pack = jnp.concatenate([along_z[:, :BLK, :].reshape(NZL * BLK, BLK), tails], axis=0)
    line = to_all(pack, AXES, 4, lines("yx"))
    plane = to_all(line.reshape(4 * PIECE, BLK), AXES, 4, lines("xy")).reshape(16 * PIECE, BLK)
    other = lax.ppermute(plane, "c", [(0, 1), (1, 0)])

    def places_of(part):
        part = part.reshape(16, PIECE, BLK)[:, NZL * BLK : NZL * BLK + NZL, :2]
        return part.astype(jnp.int32).reshape(-1)

    cand = cand_blocks.reshape(-1)
    fsdp = (me["y"] * NZL + me["zl"]) * NC + me["c"]
    info = jnp.stack([fsdp * rows_dev, group_counts[0]]).astype(jnp.int32)
    first = first_half(tokens, plane, places_of(plane), cand, out_grad.shape[1] // BLK)
    partial = second_half(tokens, out_grad, other, first, places_of(other), cand, info)
    pair = lax.all_to_all(partial, "c", 0, 0, tiled=True)
    mine = jnp.sum(pair.astype(jnp.float32), axis=0).astype(jnp.bfloat16)
    mine = mine.reshape(NX * NY, NZL, BLK // NX, BLK)
    planes = lax.all_to_all(mine, ("x", "y"), 0, 0, tiled=True)
    strip = jnp.sum(planes.astype(jnp.float32), axis=0).astype(jnp.bfloat16)
    strips = jnp.broadcast_to(strip[None], (NZH,) + strip.shape).reshape(NZH * NZL, BLK // NX, BLK)
    strips = lax.all_to_all(strips, ("zh", "zl"), 0, 0, tiled=True)
    summed = jnp.sum(strips.astype(jnp.float32), axis=0)
    whole = to_all(summed, "x", NX).reshape(1, BLK, BLK)
    scale = (rows_dev * NX * NZH * NY * NZL * NC) ** (-0.5)
    cand_grad = whole * scale
    cand_score = jnp.sqrt(jnp.mean(cand_grad * cand_grad, axis=(1, 2)) + 1e-06)
    return (cand_grad, cand_score)


def solution(mesh):
    fine = Mesh(mesh.devices.reshape(SIZES), AXES)
    dp, fsdp = ("x", "zh"), ("y", "zl", "c")
    return jax.shard_map(
        per_device,
        mesh=fine,
        in_specs=(
            P(AXES, None),
            P(AXES, None),
            P(fsdp, None, None),
            P(fsdp, None),
            P(fsdp),
            P(),
            P(dp),
        ),
        out_specs=(P(fsdp, None, None), P(fsdp)),
        check_vma=False,
    )
```

```python
import jax
import jax.numpy as jnp
from jax import lax
from jax.experimental import pallas as pl
from jax.experimental.pallas import tpu as pltpu
from jax.sharding import Mesh, PartitionSpec as P

AXES = ("x", "zh", "y", "zl", "c")
SIZES = (4, 2, 4, 8, 2)
NX, NZH, NY, NZL, NC = SIZES
BLK = 128
TAIL = 16
PIECE = NZL * BLK + TAIL
MUL = 8
LIMIT1 = 20
LIMIT2 = 24


def flat(x, zh, y, zl, c):
    return (((x * NZH + zh) * NY + y) * NZL + zl) * NC + c


def runs_along_z():
    return [
        [flat(x, (z // NZL) % NZH, y, z % NZL, c) for z in range(start, start + NZL)]
        for c in range(NC)
        for x in range(NX)
        for y in range(NY)
        for start in (4 * c, 4 * c + NZL)
    ]


def lines(axis_of_core):
    groups = []
    for c, axis in enumerate(axis_of_core):
        for zh in range(NZH):
            for zl in range(NZL):
                for other in range(4):
                    if axis == "y":
                        groups.append([flat(other, zh, y, zl, c) for y in range(NY)])
                    else:
                        groups.append([flat(x, zh, other, zl, c) for x in range(NX)])
    return groups


def to_all(value, axis, count, groups=None):
    copies = jnp.broadcast_to(value[None], (count,) + value.shape)
    return lax.all_to_all(copies, axis, 0, 0, axis_index_groups=groups, tiled=True)


def gelu_slope(value_in):
    normal_cdf = 0.5 * (1.0 + lax.erf(value_in * 0.7071067811865476))
    density = jnp.exp(-0.5 * value_in * value_in) * 0.3989422804014327
    return normal_cdf + value_in * density


def tails_copy(pack_hbm, tails, sem):
    return pltpu.make_async_copy(pack_hbm.at[:, pl.ds(NZL * BLK, TAIL), :], tails, sem)


def read_places(tails, numbers, places, sem):
    row = lax.broadcasted_iota(jnp.int32, (TAIL, BLK), 0)
    table = jnp.zeros((TAIL, BLK), jnp.float32)
    for p in range(tails.shape[0]):
        table = jnp.where(row == p, tails[p].astype(jnp.float32), table)
    numbers[...] = table.astype(jnp.int32)
    move = pltpu.make_async_copy(numbers, places, sem)
    move.start()
    move.wait()


def choose_blocks(places, slot_of, rows, slots, offs, spare, unroll):
    def choose(pack, count):
        found = [places[pack, 2 * z + 1] for z in range(NZL)]
        found = [slot_of[col] for col in found]
        where = [places[pack, 2 * z] for z in range(NZL)]
        for z in range(NZL):
            rows[count] = where[z]
            slots[count] = found[z]
            offs[count] = pack * NZL + z
            count = count + (found[z] != spare).astype(jnp.int32)
        return count

    count = lax.fori_loop(0, places.shape[0], choose, 0, unroll=2)
    for u in range(unroll):
        rows[count + u] = 0
        slots[count + u] = spare
        offs[count + u] = 0
    return count


def give_slots(cand, slot_of, spare):
    def clear(i, carry):
        slot_of[i] = spare
        return carry

    lax.fori_loop(0, slot_of.shape[0], clear, 0, unroll=8)

    def mark(j, count):
        col = cand[1, j]
        had = slot_of[col]
        fresh = had == spare
        slot_of[col] = jnp.where(fresh, count, had)
        return count + fresh.astype(jnp.int32)

    return lax.fori_loop(0, cand.shape[1], mark, 0, unroll=4)


def add_products(count, tok_ref, weights, acc, rows, slots, offs, unroll):
    def multiply(step, carry):
        products = []
        for u in range(unroll):
            i = step * unroll + u
            row = pl.multiple_of(rows[i] * BLK, BLK)
            pack = offs[i] // NZL
            off = pl.multiple_of(offs[i] % NZL * BLK, BLK)
            products.append(
                jnp.dot(
                    tok_ref[:, pl.ds(row, BLK)],
                    weights[pack, pl.ds(off, BLK), :],
                    preferred_element_type=jnp.float32,
                )
            )
        for u in range(unroll):
            acc[slots[step * unroll + u]] += products[u]
        return carry

    lax.fori_loop(0, (count + unroll - 1) // unroll, multiply, 0)


def piece_kernel(drop, active, blocks, out_ref, block, sem):
    slot = lax.axis_index("x")
    slot = slot + (slot >= drop[0]).astype(jnp.int32)
    fetch = pltpu.make_async_copy(blocks.at[slot], block, sem)
    fetch.start()
    lane = lax.broadcasted_iota(jnp.int32, (TAIL, BLK), 1)
    spot = 2 * ((lax.axis_index("zl") + 4 * lax.axis_index("c")) % NZL)
    tail = jnp.where(lane == spot, active[0, slot], 0)
    tail = jnp.where(lane == spot + 1, active[1, slot], tail)
    tail = tail.astype(jnp.float32).astype(jnp.bfloat16)
    for e in range(NZL):
        out_ref[e, pl.ds(BLK, TAIL), :] = tail
    fetch.wait()
    for e in range(NZL):
        out_ref[e, pl.ds(0, BLK), :] = block[...]


def first_pieces(drop, active, blocks):
    return pl.pallas_call(
        piece_kernel,
        out_shape=jax.ShapeDtypeStruct((NZL, BLK + TAIL, BLK), jnp.bfloat16),
        grid_spec=pltpu.PrefetchScalarGridSpec(
            num_scalar_prefetch=2,
            grid=(),
            in_specs=[ANY],
            out_specs=VMEM,
            scratch_shapes=[pltpu.VMEM((BLK, BLK), jnp.bfloat16), pltpu.SemaphoreType.DMA],
        ),
        compiler_params=pltpu.CompilerParams(vmem_limit_bytes=16 * 1024 * 1024),
    )(drop, active, blocks)


def first_kernel(
    cand, tok_ref, own_hbm, acc,
    weights, tails, numbers, places, slot_of, rows, slots, offs, sem,
):
    copy_own = pltpu.make_async_copy(own_hbm, weights, sem.at[0])
    copy_tails = tails_copy(own_hbm, tails, sem.at[1])
    copy_tails.start()
    copy_own.start()
    spare = acc.shape[0] - 1
    give_slots(cand, slot_of, spare)

    copy_tails.wait()
    read_places(tails, numbers, places, sem.at[1])

    def zero(i, carry):
        acc[i] = jnp.zeros(acc.shape[1:], jnp.float32)
        return carry

    lax.fori_loop(0, spare + 1, zero, 0, unroll=5)
    count = choose_blocks(places, slot_of, rows, slots, offs, spare, MUL)
    copy_own.wait()
    add_products(count, tok_ref, weights, acc, rows, slots, offs, MUL)


def second_kernel(
    cand, info, tok_ref, other_hbm, first, grad_ref, send_ref, keep_ref,
    weights, acc, tails, numbers, places, slot_of, rows, slots, offs, sem,
):
    copy_other = pltpu.make_async_copy(other_hbm, weights, sem.at[0])
    copy_tails = tails_copy(other_hbm, tails, sem.at[1])
    copy_tails.start()
    copy_other.start()
    spare = acc.shape[0] - 1
    tokens = tok_ref.shape[0]
    give_slots(cand, slot_of, spare)

    def zero(i, carry):
        acc[i] = jnp.zeros(acc.shape[1:], jnp.float32)
        return carry

    lax.fori_loop(0, spare + 1, zero, 0, unroll=5)
    copy_tails.wait()
    read_places(tails, numbers, places, sem.at[1])
    count = choose_blocks(places, slot_of, rows, slots, offs, spare, MUL)
    copy_other.wait()
    add_products(count, tok_ref, weights, acc, rows, slots, offs, MUL)
    position = info[0] + lax.broadcasted_iota(jnp.int32, (tokens, BLK), 0)
    usable = (position < info[1]).astype(jnp.float32)

    def gradient(q, carry):
        y, z = q // NZL, q % NZL
        for out_ref, core in ((send_ref, 1 - info[2]), (keep_ref, info[2])):
            j = q * NC + core
            col = cand[1, j]
            slot = slot_of[col]
            lanes = pl.ds(pl.multiple_of(col * BLK, BLK), BLK)
            slope = gelu_slope(first[slot] + acc[slot])
            given = grad_ref[:, lanes].astype(jnp.float32)
            row = pl.multiple_of(cand[0, j] * BLK, BLK)
            part = lax.dot_general(
                tok_ref[:, pl.ds(row, BLK)],
                (given * slope * usable).astype(jnp.bfloat16),
                (((0,), (0,)), ((), ())),
                preferred_element_type=jnp.float32,
            ).astype(jnp.bfloat16)
            for x in range(NX):
                out_ref[x, y, z] = part[x * 32 : (x + 1) * 32]
        return carry

    lax.fori_loop(0, cand.shape[1] // NC, gradient, 0, unroll=4)


def place_scratch(packs):
    return [
        pltpu.VMEM((packs, TAIL, BLK), jnp.bfloat16),
        pltpu.VMEM((TAIL, BLK), jnp.int32),
        pltpu.SMEM((TAIL, BLK), jnp.int32),
    ]


def lists(cols, stored):
    smem = lambda count: pltpu.SMEM((count,), jnp.int32)
    return [smem(cols)] + [smem(stored + 2 * MUL)] * 3


VMEM = pl.BlockSpec(memory_space=pltpu.VMEM)
ANY = pl.BlockSpec(memory_space=pl.ANY)


def first_half(tokens, own, cand, col_blocks):
    packs, cands = own.shape[0], cand.shape[1]
    rows_dev = tokens.shape[0]
    return pl.pallas_call(
        first_kernel,
        out_shape=jax.ShapeDtypeStruct((cands + 1, rows_dev, BLK), jnp.float32),
        grid_spec=pltpu.PrefetchScalarGridSpec(
            num_scalar_prefetch=1,
            grid=(),
            in_specs=[VMEM, ANY],
            out_specs=VMEM,
            scratch_shapes=[pltpu.VMEM(own.shape, jnp.bfloat16)]
            + place_scratch(packs)
            + lists(col_blocks, packs * NZL)
            + [pltpu.SemaphoreType.DMA((2,))],
        ),
        compiler_params=pltpu.CompilerParams(vmem_limit_bytes=LIMIT1 * 1024 * 1024),
        cost_estimate=pl.CostEstimate(
            flops=2 * packs * NZL * rows_dev * BLK * BLK,
            bytes_accessed=10_000_000,
            transcendentals=0,
        ),
    )(cand, tokens, own)


def second_half(tokens, other, first, out_grad, cand, info):
    packs, cands = other.shape[0], cand.shape[1]
    col_blocks = out_grad.shape[1] // BLK
    rows_dev = tokens.shape[0]
    part = jax.ShapeDtypeStruct((NX, NY, NZL, BLK // NX, BLK), jnp.bfloat16)
    return pl.pallas_call(
        second_kernel,
        out_shape=(part, part),
        grid_spec=pltpu.PrefetchScalarGridSpec(
            num_scalar_prefetch=2,
            grid=(),
            in_specs=[VMEM, ANY, VMEM, VMEM],
            out_specs=(VMEM, VMEM),
            scratch_shapes=[
                pltpu.VMEM(other.shape, jnp.bfloat16),
                pltpu.VMEM((cands + 1, rows_dev, BLK), jnp.float32),
            ]
            + place_scratch(packs)
            + lists(col_blocks, packs * NZL)
            + [pltpu.SemaphoreType.DMA((2,))],
        ),
        compiler_params=pltpu.CompilerParams(vmem_limit_bytes=LIMIT2 * 1024 * 1024),
        cost_estimate=pl.CostEstimate(
            flops=2 * (packs * NZL + cands) * rows_dev * BLK * BLK,
            bytes_accessed=15_000_000,
            transcendentals=2_000_000,
        ),
    )(cand, info, tokens, other, first, out_grad)


def per_device(
    tokens, out_grad, block_values, active_blocks, drop_slots, cand_blocks, group_counts
):
    rows_dev = tokens.shape[0]
    me = {name: lax.axis_index(name) for name in AXES}
    pieces = first_pieces(drop_slots, active_blocks.T, block_values)
    along_z = lax.all_to_all(
        pieces, AXES, 0, 0, axis_index_groups=runs_along_z(), tiled=True
    )
    tail = jnp.sum(along_z[:, BLK:, :], axis=0)
    pack = jnp.concatenate([along_z[:, :BLK, :].reshape(NZL * BLK, BLK), tail], axis=0)
    line = to_all(pack, AXES, 4, lines("yx"))
    plane = to_all(line.reshape(4 * PIECE, BLK), AXES, 4, lines("xy")).reshape(16, PIECE, BLK)
    other = lax.ppermute(plane, "c", [(0, 1), (1, 0)])
    cand = cand_blocks.T
    fsdp = (me["y"] * NZL + me["zl"]) * NC + me["c"]
    info = jnp.stack([fsdp * rows_dev, group_counts[0], me["c"]]).astype(jnp.int32)
    first = first_half(tokens, plane, cand, out_grad.shape[1] // BLK)
    send, keep = second_half(tokens, other, first, out_grad, cand, info)
    given = lax.ppermute(send, "c", [(0, 1), (1, 0)])
    mine = (keep.astype(jnp.float32) + given.astype(jnp.float32)).astype(jnp.bfloat16)
    mine = mine.reshape(NX * NY, NZL, BLK // NX, BLK)
    planes = lax.all_to_all(mine, ("x", "y"), 0, 0, tiled=True)
    strip = jnp.sum(planes.astype(jnp.float32), axis=0).astype(jnp.bfloat16)
    strips = jnp.broadcast_to(strip[None], (NZH,) + strip.shape).reshape(NZH * NZL, BLK // NX, BLK)
    strips = lax.all_to_all(strips, ("zh", "zl"), 0, 0, tiled=True)
    summed = jnp.sum(strips.astype(jnp.float32), axis=0)
    whole = to_all(summed, "x", NX).reshape(1, BLK, BLK)
    scale = (rows_dev * NX * NZH * NY * NZL * NC) ** (-0.5)
    cand_grad = whole * scale
    cand_score = jnp.sqrt(jnp.mean(cand_grad * cand_grad, axis=(1, 2)) + 1e-06)
    return (cand_grad, cand_score)


def solution(mesh):
    fine = Mesh(mesh.devices.reshape(SIZES), AXES)
    dp, fsdp = ("x", "zh"), ("y", "zl", "c")
    return jax.shard_map(
        per_device,
        mesh=fine,
        in_specs=(
            P(AXES, None),
            P(AXES, None),
            P(fsdp, None, None),
            P(fsdp, None),
            P(fsdp),
            P(),
            P(dp),
        ),
        out_specs=(P(fsdp, None, None), P(fsdp)),
        check_vma=False,
    )
```

```python
import functools

import jax
import jax.numpy as jnp
from jax import lax
from jax.experimental import pallas as pl
from jax.experimental.pallas import tpu as pltpu
from jax.sharding import Mesh, PartitionSpec as P

AXES = ("x", "zh", "y", "zl", "c")
SIZES = (4, 2, 4, 8, 2)
NX, NZH, NY, NZL, NC = SIZES
BLK = 128
TAIL = 16
PIECE = NZL * BLK + TAIL
MUL = 8
LIMIT1 = 20
LIMIT2 = 24


def flat(x, zh, y, zl, c):
    return (((x * NZH + zh) * NY + y) * NZL + zl) * NC + c


def runs_along_z():
    return [
        [flat(x, (z // NZL) % NZH, y, z % NZL, c) for z in range(start, start + NZL)]
        for c in range(NC)
        for x in range(NX)
        for y in range(NY)
        for start in (4 - 4 * c, 4 - 4 * c + NZL)
    ]


def shift(groups, by):
    return [(group[i], group[(i + by) % 4]) for group in groups for i in range(4)]


def lines(axis_of_core):
    groups = []
    for c, axis in enumerate(axis_of_core):
        for zh in range(NZH):
            for zl in range(NZL):
                for other in range(4):
                    if axis == "y":
                        groups.append([flat(other, zh, y, zl, c) for y in range(NY)])
                    else:
                        groups.append([flat(x, zh, other, zl, c) for x in range(NX)])
    return groups


def to_all(value, axis, count, groups=None):
    copies = jnp.broadcast_to(value[None], (count,) + value.shape)
    return lax.all_to_all(copies, axis, 0, 0, axis_index_groups=groups, tiled=True)


def gelu_slope(value_in):
    normal_cdf = 0.5 * (1.0 + lax.erf(value_in * 0.7071067811865476))
    density = jnp.exp(-0.5 * value_in * value_in) * 0.3989422804014327
    return normal_cdf + value_in * density


def read_places(tails, numbers, places, sem):
    row = lax.broadcasted_iota(jnp.int32, (TAIL, BLK), 0)
    table = jnp.zeros((TAIL, BLK), jnp.float32)
    for p in range(tails.shape[0]):
        table = jnp.where(row == p, tails[p].astype(jnp.float32), table)
    numbers[...] = table.astype(jnp.int32)
    move = pltpu.make_async_copy(numbers, places, sem)
    move.start()
    move.wait()


def choose_blocks(packs, places, slot_of, rows, slots, offs, spare, unroll):
    def choose(pack, count):
        found = [places[pack, 2 * z + 1] for z in range(NZL)]
        found = [slot_of[col] for col in found]
        where = [places[pack, 2 * z] for z in range(NZL)]
        for z in range(NZL):
            rows[count] = where[z]
            slots[count] = found[z]
            offs[count] = pack * NZL + z
            count = count + (found[z] != spare).astype(jnp.int32)
        return count

    count = lax.fori_loop(0, packs, choose, 0, unroll=2)
    for u in range(unroll):
        rows[count + u] = 0
        slots[count + u] = spare
        offs[count + u] = 0
    return count


def give_slots(cand, slot_of, spare):
    def clear(i, carry):
        slot_of[i] = spare
        return carry

    lax.fori_loop(0, slot_of.shape[0], clear, 0, unroll=8)

    def mark(j, count):
        col = cand[1, j]
        had = slot_of[col]
        fresh = had == spare
        slot_of[col] = jnp.where(fresh, count, had)
        return count + fresh.astype(jnp.int32)

    return lax.fori_loop(0, cand.shape[1], mark, 0, unroll=4)


def add_products(count, tok_ref, weights, acc, rows, slots, offs, unroll):
    def multiply(step, carry):
        products = []
        for u in range(unroll):
            i = step * unroll + u
            row = pl.multiple_of(rows[i] * BLK, BLK)
            pack = offs[i] // NZL
            off = pl.multiple_of(offs[i] % NZL * BLK, BLK)
            products.append(
                jnp.dot(
                    tok_ref[:, pl.ds(row, BLK)],
                    weights[pack, pl.ds(off, BLK), :],
                    preferred_element_type=jnp.float32,
                )
            )
        for u in range(unroll):
            acc[slots[step * unroll + u]] += products[u]
        return carry

    lax.fori_loop(0, (count + unroll - 1) // unroll, multiply, 0)


def piece_kernel(drop, active, blocks, out_ref, block, sem):
    slot = lax.axis_index("x")
    slot = slot + (slot >= drop[0]).astype(jnp.int32)
    fetch = pltpu.make_async_copy(blocks.at[slot], block, sem)
    fetch.start()
    lane = lax.broadcasted_iota(jnp.int32, (TAIL, BLK), 1)
    spot = 2 * ((lax.axis_index("zl") + 4 - 4 * lax.axis_index("c")) % NZL)
    tail = jnp.where(lane == spot, active[0, slot], 0)
    tail = jnp.where(lane == spot + 1, active[1, slot], tail)
    tail = tail.astype(jnp.float32).astype(jnp.bfloat16)
    for e in range(NZL):
        out_ref[e, pl.ds(BLK, TAIL), :] = tail
    fetch.wait()
    for e in range(NZL):
        out_ref[e, pl.ds(0, BLK), :] = block[...]


def first_pieces(drop, active, blocks):
    return pl.pallas_call(
        piece_kernel,
        out_shape=jax.ShapeDtypeStruct((NZL, BLK + TAIL, BLK), jnp.bfloat16),
        grid_spec=pltpu.PrefetchScalarGridSpec(
            num_scalar_prefetch=2,
            grid=(),
            in_specs=[ANY],
            out_specs=VMEM,
            scratch_shapes=[pltpu.VMEM((BLK, BLK), jnp.bfloat16), pltpu.SemaphoreType.DMA],
        ),
        compiler_params=pltpu.CompilerParams(vmem_limit_bytes=16 * 1024 * 1024),
    )(drop, active, blocks)


def fetch_pieces(pieces, weights, tails, sem, tail_sem):
    blocks, ends, at = [], [], 0
    for i, piece in enumerate(pieces):
        span = pl.ds(at, piece.shape[0])
        ends.append(
            pltpu.make_async_copy(
                piece.at[:, pl.ds(NZL * BLK, TAIL), :], tails.at[span], tail_sem.at[i]
            )
        )
        blocks.append(pltpu.make_async_copy(piece, weights.at[span], sem.at[i]))
        at += piece.shape[0]
    for copy in ends + blocks:
        copy.start()

    def wait(copies):
        for copy in copies:
            copy.wait()

    return functools.partial(wait, ends), functools.partial(wait, blocks)


def add_kernel(count, later, cand, tok_ref, *refs):
    pieces, refs = refs[:count], refs[count:]
    if later:
        before, refs = refs[0], refs[1:]
    (acc, weights, tails, numbers, places, slot_of, rows, slots, offs,
     sem, tail_sem, move_sem) = refs
    wait_tails, wait_blocks = fetch_pieces(pieces, weights, tails, sem, tail_sem)
    spare = acc.shape[0] - 1
    give_slots(cand, slot_of, spare)

    def begin(i, carry):
        acc[i] = before[i] if later else jnp.zeros(acc.shape[1:], jnp.float32)
        return carry

    lax.fori_loop(0, spare + 1, begin, 0, unroll=5)
    wait_tails()
    read_places(tails, numbers, places, move_sem)
    found = choose_blocks(tails.shape[0], places, slot_of, rows, slots, offs, spare, MUL)
    wait_blocks()
    add_products(found, tok_ref, weights, acc, rows, slots, offs, MUL)


def second_kernel(
    cand, counts, tok_ref, one, two, first, grad_ref, send_ref, keep_ref,
    weights, acc, tails, numbers, places, slot_of, rows, slots, offs, sem, tail_sem, move_sem,
):
    wait_tails, wait_blocks = fetch_pieces([one, two], weights, tails, sem, tail_sem)
    spare = acc.shape[0] - 1
    tokens = tok_ref.shape[0]
    give_slots(cand, slot_of, spare)

    def zero(i, carry):
        acc[i] = jnp.zeros(acc.shape[1:], jnp.float32)
        return carry

    lax.fori_loop(0, spare + 1, zero, 0, unroll=5)
    wait_tails()
    read_places(tails, numbers, places, move_sem)
    found = choose_blocks(tails.shape[0], places, slot_of, rows, slots, offs, spare, MUL)
    wait_blocks()
    add_products(found, tok_ref, weights, acc, rows, slots, offs, MUL)
    core_here = lax.axis_index("c")
    index = (lax.axis_index("y") * NZL + lax.axis_index("zl")) * NC + core_here
    position = index * tokens + lax.broadcasted_iota(jnp.int32, (tokens, BLK), 0)
    usable = (position < counts[0]).astype(jnp.float32)

    def gradient(q, carry):
        y, z = q // NZL, q % NZL
        for out_ref, core in ((send_ref, 1 - core_here), (keep_ref, core_here)):
            j = q * NC + core
            col = cand[1, j]
            slot = slot_of[col]
            lanes = pl.ds(pl.multiple_of(col * BLK, BLK), BLK)
            slope = gelu_slope(first[slot] + acc[slot])
            given = grad_ref[:, lanes].astype(jnp.float32)
            row = pl.multiple_of(cand[0, j] * BLK, BLK)
            part = lax.dot_general(
                tok_ref[:, pl.ds(row, BLK)],
                (given * slope * usable).astype(jnp.bfloat16),
                (((0,), (0,)), ((), ())),
                preferred_element_type=jnp.float32,
            ).astype(jnp.bfloat16)
            for x in range(NX):
                out_ref[x, y, z] = part[x * 32 : (x + 1) * 32]
        return carry

    lax.fori_loop(0, cand.shape[1] // NC, gradient, 0, unroll=4)


def place_scratch(packs):
    return [
        pltpu.VMEM((packs, TAIL, BLK), jnp.bfloat16),
        pltpu.VMEM((TAIL, BLK), jnp.int32),
        pltpu.SMEM((TAIL, BLK), jnp.int32),
    ]


def lists(cols, stored):
    smem = lambda count: pltpu.SMEM((count,), jnp.int32)
    return [smem(cols)] + [smem(stored + 2 * MUL)] * 3


VMEM = pl.BlockSpec(memory_space=pltpu.VMEM)
ANY = pl.BlockSpec(memory_space=pl.ANY)


def add_pieces(tokens, pieces, cand, col_blocks, before=None):
    packs, cands = sum(piece.shape[0] for piece in pieces), cand.shape[1]
    rows_dev, count = tokens.shape[0], len(pieces)
    later = before is not None
    return pl.pallas_call(
        functools.partial(add_kernel, count, later),
        out_shape=jax.ShapeDtypeStruct((cands + 1, rows_dev, BLK), jnp.float32),
        grid_spec=pltpu.PrefetchScalarGridSpec(
            num_scalar_prefetch=1,
            grid=(),
            in_specs=[VMEM] + [ANY] * count + [VMEM] * later,
            out_specs=VMEM,
            scratch_shapes=[pltpu.VMEM((packs, PIECE, BLK), jnp.bfloat16)]
            + place_scratch(packs)
            + lists(col_blocks, packs * NZL)
            + [pltpu.SemaphoreType.DMA((count,))] * 2
            + [pltpu.SemaphoreType.DMA],
        ),
        compiler_params=pltpu.CompilerParams(vmem_limit_bytes=LIMIT1 * 1024 * 1024),
        cost_estimate=pl.CostEstimate(
            flops=2 * packs * NZL * rows_dev * BLK * BLK,
            bytes_accessed=10_000_000,
            transcendentals=0,
        ),
    )(cand, tokens, *pieces, *([before] if later else []))


def second_half(tokens, pieces, first, out_grad, cand, counts):
    packs, cands = sum(piece.shape[0] for piece in pieces), cand.shape[1]
    col_blocks = out_grad.shape[1] // BLK
    rows_dev = tokens.shape[0]
    part = jax.ShapeDtypeStruct((NX, NY, NZL, BLK // NX, BLK), jnp.bfloat16)
    return pl.pallas_call(
        second_kernel,
        out_shape=(part, part),
        grid_spec=pltpu.PrefetchScalarGridSpec(
            num_scalar_prefetch=2,
            grid=(),
            in_specs=[VMEM, ANY, ANY, VMEM, VMEM],
            out_specs=(VMEM, VMEM),
            scratch_shapes=[
                pltpu.VMEM((packs, PIECE, BLK), jnp.bfloat16),
                pltpu.VMEM((cands + 1, rows_dev, BLK), jnp.float32),
            ]
            + place_scratch(packs)
            + lists(col_blocks, packs * NZL)
            + [pltpu.SemaphoreType.DMA((2,))] * 2 + [pltpu.SemaphoreType.DMA],
        ),
        compiler_params=pltpu.CompilerParams(vmem_limit_bytes=LIMIT2 * 1024 * 1024),
        cost_estimate=pl.CostEstimate(
            flops=2 * (packs * NZL + cands) * rows_dev * BLK * BLK,
            bytes_accessed=15_000_000,
            transcendentals=2_000_000,
        ),
    )(cand, counts, tokens, *pieces, first, out_grad)


def per_device(
    tokens, out_grad, block_values, active_blocks, drop_slots, cand_blocks, group_counts
):
    rows_dev = tokens.shape[0]
    pieces = first_pieces(drop_slots, active_blocks.T, block_values)
    along_z = lax.all_to_all(
        pieces, AXES, 0, 0, axis_index_groups=runs_along_z(), tiled=True
    )
    tail = jnp.sum(along_z[:, BLK:, :], axis=0)
    pack = jnp.concatenate([along_z[:, :BLK, :].reshape(NZL * BLK, BLK), tail], axis=0)
    line = to_all(pack, AXES, 4, lines("yx"))
    cand = cand_blocks.T
    rings = lines("xy")
    swap = [(i, i ^ 1) for i in range(NX * NZH * NY * NZL * NC)]

    def swapped(value):
        return lax.ppermute(value, AXES, swap)

    cols = out_grad.shape[1] // BLK
    one, two, three = (lax.ppermute(line, AXES, shift(rings, by)) for by in (2, 1, 3))
    line_other = swapped(line)
    acc = add_pieces(tokens, [line], cand, cols)
    one, acc = lax.optimization_barrier((one, acc))
    one_other = swapped(one)
    acc = add_pieces(tokens, [one, line_other], cand, cols, acc)
    two, three, acc = lax.optimization_barrier((two, three, acc))
    two_other, three_other = swapped(two), swapped(three)
    acc = add_pieces(tokens, [two, three, one_other], cand, cols, acc)
    send, keep = second_half(tokens, [two_other, three_other], acc, out_grad, cand, group_counts)
    given = lax.ppermute(send, "c", [(0, 1), (1, 0)])
    mine = (keep.astype(jnp.float32) + given.astype(jnp.float32)).astype(jnp.bfloat16)
    mine = mine.reshape(NX * NY, NZL, BLK // NX, BLK)
    planes = lax.all_to_all(mine, ("x", "y"), 0, 0, tiled=True)
    strip = jnp.sum(planes.astype(jnp.float32), axis=0).astype(jnp.bfloat16)
    strips = jnp.broadcast_to(strip[None], (NZH,) + strip.shape).reshape(NZH * NZL, BLK // NX, BLK)
    strips = lax.all_to_all(strips, ("zh", "zl"), 0, 0, tiled=True)
    summed = jnp.sum(strips.astype(jnp.float32), axis=0)
    whole = to_all(summed, "x", NX).reshape(1, BLK, BLK)
    scale = (rows_dev * NX * NZH * NY * NZL * NC) ** (-0.5)
    cand_grad = whole * scale
    cand_score = jnp.sqrt(jnp.mean(cand_grad * cand_grad, axis=(1, 2)) + 1e-06)
    return (cand_grad, cand_score)


def solution(mesh):
    fine = Mesh(mesh.devices.reshape(SIZES), AXES)
    dp, fsdp = ("x", "zh"), ("y", "zl", "c")
    return jax.shard_map(
        per_device,
        mesh=fine,
        in_specs=(
            P(AXES, None),
            P(AXES, None),
            P(fsdp, None, None),
            P(fsdp, None),
            P(fsdp),
            P(),
            P(dp),
        ),
        out_specs=(P(fsdp, None, None), P(fsdp)),
        check_vma=False,
    )
```

```python
import functools

import jax
import jax.numpy as jnp
from jax import lax
from jax.experimental import pallas as pl
from jax.experimental.pallas import tpu as pltpu
from jax.sharding import Mesh, PartitionSpec as P

AXES = ("x", "zh", "y", "zl", "c")
SIZES = (4, 2, 4, 8, 2)
NX, NZH, NY, NZL, NC = SIZES
BLK = 128
TAIL = 16
PIECE = NZL * BLK + TAIL
MUL = 8
LIMIT1 = 20
LIMIT2 = 24


def flat(x, zh, y, zl, c):
    return (((x * NZH + zh) * NY + y) * NZL + zl) * NC + c


def runs_along_z():
    return [
        [flat(x, (z // NZL) % NZH, y, z % NZL, c) for z in range(start, start + NZL)]
        for c in range(NC)
        for x in range(NX)
        for y in range(NY)
        for start in (4 - 4 * c, 4 - 4 * c + NZL)
    ]


def shift(groups, by):
    return [(group[i], group[(i + by) % 4]) for group in groups for i in range(4)]


def lines(axis_of_core):
    groups = []
    for c, axis in enumerate(axis_of_core):
        for zh in range(NZH):
            for zl in range(NZL):
                for other in range(4):
                    if axis == "y":
                        groups.append([flat(other, zh, y, zl, c) for y in range(NY)])
                    else:
                        groups.append([flat(x, zh, other, zl, c) for x in range(NX)])
    return groups


def to_all(value, axis, count, groups=None):
    copies = jnp.broadcast_to(value[None], (count,) + value.shape)
    return lax.all_to_all(copies, axis, 0, 0, axis_index_groups=groups, tiled=True)


def gelu_slope(value_in):
    normal_cdf = 0.5 * (1.0 + lax.erf(value_in * 0.7071067811865476))
    density = jnp.exp(-0.5 * value_in * value_in) * 0.3989422804014327
    return normal_cdf + value_in * density


def read_places(tails, numbers, places, sem):
    row = lax.broadcasted_iota(jnp.int32, (TAIL, BLK), 0)
    table = jnp.zeros((TAIL, BLK), jnp.float32)
    for p in range(tails.shape[0]):
        table = jnp.where(row == p, tails[p].astype(jnp.float32), table)
    numbers[...] = table.astype(jnp.int32)
    move = pltpu.make_async_copy(numbers, places, sem)
    move.start()
    move.wait()


def choose_blocks(packs, places, slot_of, rows, slots, offs, spare, unroll):
    def choose(pack, count):
        found = [places[pack, 2 * z + 1] for z in range(NZL)]
        found = [slot_of[col] for col in found]
        where = [places[pack, 2 * z] for z in range(NZL)]
        for z in range(NZL):
            rows[count] = where[z]
            slots[count] = found[z]
            offs[count] = pack * NZL + z
            count = count + (found[z] != spare).astype(jnp.int32)
        return count

    count = lax.fori_loop(0, packs, choose, 0, unroll=2)
    for u in range(unroll):
        rows[count + u] = 0
        slots[count + u] = spare
        offs[count + u] = 0
    return count


def give_slots(cand, slot_of, spare):
    def clear(i, carry):
        slot_of[i] = spare
        return carry

    lax.fori_loop(0, slot_of.shape[0], clear, 0, unroll=8)

    def mark(j, count):
        col = cand[1, j]
        had = slot_of[col]
        fresh = had == spare
        slot_of[col] = jnp.where(fresh, count, had)
        return count + fresh.astype(jnp.int32)

    return lax.fori_loop(0, cand.shape[1], mark, 0, unroll=4)


def add_products(count, tok_ref, weights, acc, rows, slots, offs, unroll):
    def multiply(step, carry):
        products = []
        for u in range(unroll):
            i = step * unroll + u
            row = pl.multiple_of(rows[i] * BLK, BLK)
            pack = offs[i] // NZL
            off = pl.multiple_of(offs[i] % NZL * BLK, BLK)
            products.append(
                jnp.dot(
                    tok_ref[:, pl.ds(row, BLK)],
                    weights[pack, pl.ds(off, BLK), :],
                    preferred_element_type=jnp.float32,
                )
            )
        for u in range(unroll):
            acc[slots[step * unroll + u]] += products[u]
        return carry

    lax.fori_loop(0, (count + unroll - 1) // unroll, multiply, 0)


def piece_kernel(drop, active, blocks, out_ref, block, sem):
    slot = lax.axis_index("x")
    slot = slot + (slot >= drop[0]).astype(jnp.int32)
    fetch = pltpu.make_async_copy(blocks.at[slot], block, sem)
    fetch.start()
    lane = lax.broadcasted_iota(jnp.int32, (TAIL, BLK), 1)
    spot = 2 * ((lax.axis_index("zl") + 4 - 4 * lax.axis_index("c")) % NZL)
    tail = jnp.where(lane == spot, active[0, slot], 0)
    tail = jnp.where(lane == spot + 1, active[1, slot], tail)
    tail = tail.astype(jnp.float32).astype(jnp.bfloat16)
    for e in range(NZL):
        out_ref[e, pl.ds(BLK, TAIL), :] = tail
    fetch.wait()
    for e in range(NZL):
        out_ref[e, pl.ds(0, BLK), :] = block[...]


def first_pieces(drop, active, blocks):
    return pl.pallas_call(
        piece_kernel,
        out_shape=jax.ShapeDtypeStruct((NZL, BLK + TAIL, BLK), jnp.bfloat16),
        grid_spec=pltpu.PrefetchScalarGridSpec(
            num_scalar_prefetch=2,
            grid=(),
            in_specs=[ANY],
            out_specs=VMEM,
            scratch_shapes=[pltpu.VMEM((BLK, BLK), jnp.bfloat16), pltpu.SemaphoreType.DMA],
        ),
        compiler_params=pltpu.CompilerParams(vmem_limit_bytes=16 * 1024 * 1024),
    )(drop, active, blocks)


def fetch_pieces(pieces, weights, tails, sem, tail_sem):
    blocks, ends, at = [], [], 0
    for i, piece in enumerate(pieces):
        span = pl.ds(at, piece.shape[0])
        ends.append(
            pltpu.make_async_copy(
                piece.at[:, pl.ds(NZL * BLK, TAIL), :], tails.at[span], tail_sem.at[i]
            )
        )
        blocks.append(pltpu.make_async_copy(piece, weights.at[span], sem.at[i]))
        at += piece.shape[0]
    for copy in ends + blocks:
        copy.start()

    def wait(copies):
        for copy in copies:
            copy.wait()

    return functools.partial(wait, ends), functools.partial(wait, blocks)


def add_kernel(count, later, cand, tok_ref, *refs):
    pieces, refs = refs[:count], refs[count:]
    if later:
        (before, acc), refs = refs[:2], refs[2:]
    else:
        (acc, turned), refs = refs[:2], refs[2:]
    (weights, tails, numbers, places, slot_of, rows, slots, offs,
     sem, tail_sem, move_sem) = refs
    wait_tails, wait_blocks = fetch_pieces(pieces, weights, tails, sem, tail_sem)
    spare = acc.shape[0] - 1
    give_slots(cand, slot_of, spare)

    def begin(i, carry):
        acc[i] = before[i] if later else jnp.zeros(acc.shape[1:], jnp.float32)
        return carry

    lax.fori_loop(0, spare + 1, begin, 0, unroll=5)
    wait_tails()
    read_places(tails, numbers, places, move_sem)
    found = choose_blocks(tails.shape[0], places, slot_of, rows, slots, offs, spare, MUL)
    if not later:
        for r in range(turned.shape[0]):
            turned[r] = tok_ref[:, r * BLK : (r + 1) * BLK].T
    wait_blocks()
    add_products(found, tok_ref, weights, acc, rows, slots, offs, MUL)


def gradients(core, cand, counts, turned, slot_of, acc, grad_ref, out_ref):
    tokens = acc.shape[1]
    index = (lax.axis_index("y") * NZL + lax.axis_index("zl")) * NC + lax.axis_index("c")
    position = index * tokens + lax.broadcasted_iota(jnp.int32, (tokens, BLK), 0)
    usable = (position < counts[0]).astype(jnp.float32)

    def gradient(q, carry):
        y, z = q // NZL, q % NZL
        j = q * NC + core
        col = cand[1, j]
        lanes = pl.ds(pl.multiple_of(col * BLK, BLK), BLK)
        slope = gelu_slope(acc[slot_of[col]])
        given = grad_ref[:, lanes].astype(jnp.float32)
        part = jnp.dot(
            turned[cand[0, j]],
            (given * slope * usable).astype(jnp.bfloat16),
            preferred_element_type=jnp.float32,
        ).astype(jnp.bfloat16)
        for x in range(NX):
            out_ref[x, y, z] = part[x * 32 : (x + 1) * 32]
        return carry

    lax.fori_loop(0, cand.shape[1] // NC, gradient, 0, unroll=8)


def second_kernel(
    cand, counts, tok_ref, turned, one, two, before, grad_ref, acc, send_ref,
    weights, tails, numbers, places, slot_of, rows, slots, offs, sem, tail_sem, move_sem,
):
    wait_tails, wait_blocks = fetch_pieces([one, two], weights, tails, sem, tail_sem)
    spare = acc.shape[0] - 1
    give_slots(cand, slot_of, spare)

    def begin(i, carry):
        acc[i] = before[i]
        return carry

    lax.fori_loop(0, spare + 1, begin, 0, unroll=5)
    wait_tails()
    read_places(tails, numbers, places, move_sem)
    found = choose_blocks(tails.shape[0], places, slot_of, rows, slots, offs, spare, MUL)
    wait_blocks()
    add_products(found, tok_ref, weights, acc, rows, slots, offs, MUL)
    gradients(
        1 - lax.axis_index("c"), cand, counts, turned, slot_of, acc, grad_ref, send_ref
    )


def third_kernel(cand, counts, turned, acc, grad_ref, keep_ref, slot_of):
    give_slots(cand, slot_of, acc.shape[0] - 1)
    gradients(lax.axis_index("c"), cand, counts, turned, slot_of, acc, grad_ref, keep_ref)


def place_scratch(packs):
    return [
        pltpu.VMEM((packs, TAIL, BLK), jnp.bfloat16),
        pltpu.VMEM((TAIL, BLK), jnp.int32),
        pltpu.SMEM((TAIL, BLK), jnp.int32),
    ]


def lists(cols, stored):
    smem = lambda count: pltpu.SMEM((count,), jnp.int32)
    return [smem(cols)] + [smem(stored + 2 * MUL)] * 3


VMEM = pl.BlockSpec(memory_space=pltpu.VMEM)
ANY = pl.BlockSpec(memory_space=pl.ANY)


def add_pieces(tokens, pieces, cand, col_blocks, before=None):
    packs, cands = sum(piece.shape[0] for piece in pieces), cand.shape[1]
    rows_dev, count = tokens.shape[0], len(pieces)
    later = before is not None
    sums = jax.ShapeDtypeStruct((cands + 1, rows_dev, BLK), jnp.float32)
    turned = jax.ShapeDtypeStruct((tokens.shape[1] // BLK, BLK, rows_dev), jnp.bfloat16)
    return pl.pallas_call(
        functools.partial(add_kernel, count, later),
        out_shape=sums if later else (sums, turned),
        grid_spec=pltpu.PrefetchScalarGridSpec(
            num_scalar_prefetch=1,
            grid=(),
            in_specs=[VMEM] + [ANY] * count + [VMEM] * later,
            out_specs=VMEM if later else (VMEM, VMEM),
            scratch_shapes=[pltpu.VMEM((packs, PIECE, BLK), jnp.bfloat16)]
            + place_scratch(packs)
            + lists(col_blocks, packs * NZL)
            + [pltpu.SemaphoreType.DMA((count,))] * 2
            + [pltpu.SemaphoreType.DMA],
        ),
        compiler_params=pltpu.CompilerParams(vmem_limit_bytes=LIMIT1 * 1024 * 1024),
        cost_estimate=pl.CostEstimate(
            flops=2 * packs * NZL * rows_dev * BLK * BLK,
            bytes_accessed=10_000_000,
            transcendentals=0,
        ),
    )(cand, tokens, *pieces, *([before] if later else []))


PART = jax.ShapeDtypeStruct((NX, NY, NZL, BLK // NX, BLK), jnp.bfloat16)


def second_half(tokens, turned, pieces, before, out_grad, cand, counts):
    packs = sum(piece.shape[0] for piece in pieces)
    col_blocks = out_grad.shape[1] // BLK
    rows_dev = tokens.shape[0]
    return pl.pallas_call(
        second_kernel,
        out_shape=(jax.ShapeDtypeStruct(before.shape, jnp.float32), PART),
        grid_spec=pltpu.PrefetchScalarGridSpec(
            num_scalar_prefetch=2,
            grid=(),
            in_specs=[VMEM, VMEM, ANY, ANY, VMEM, VMEM],
            out_specs=(VMEM, VMEM),
            scratch_shapes=[pltpu.VMEM((packs, PIECE, BLK), jnp.bfloat16)]
            + place_scratch(packs)
            + lists(col_blocks, packs * NZL)
            + [pltpu.SemaphoreType.DMA((2,))] * 2
            + [pltpu.SemaphoreType.DMA],
        ),
        compiler_params=pltpu.CompilerParams(vmem_limit_bytes=LIMIT2 * 1024 * 1024),
        cost_estimate=pl.CostEstimate(
            flops=2 * (packs * NZL + 32) * rows_dev * BLK * BLK,
            bytes_accessed=15_000_000,
            transcendentals=1_000_000,
        ),
    )(cand, counts, tokens, turned, *pieces, before, out_grad)


def third_part(turned, acc, out_grad, cand, counts):
    return pl.pallas_call(
        third_kernel,
        out_shape=PART,
        grid_spec=pltpu.PrefetchScalarGridSpec(
            num_scalar_prefetch=2,
            grid=(),
            in_specs=[VMEM, VMEM, VMEM],
            out_specs=VMEM,
            scratch_shapes=[pltpu.SMEM((out_grad.shape[1] // BLK,), jnp.int32)],
        ),
        compiler_params=pltpu.CompilerParams(vmem_limit_bytes=LIMIT2 * 1024 * 1024),
        cost_estimate=pl.CostEstimate(
            flops=2 * 32 * BLK**3, bytes_accessed=8_000_000, transcendentals=1_000_000
        ),
    )(cand, counts, turned, acc, out_grad)


def per_device(
    tokens, out_grad, block_values, active_blocks, drop_slots, cand_blocks, group_counts
):
    rows_dev = tokens.shape[0]
    pieces = first_pieces(drop_slots, active_blocks.T, block_values)
    along_z = lax.all_to_all(
        pieces, AXES, 0, 0, axis_index_groups=runs_along_z(), tiled=True
    )
    tail = jnp.sum(along_z[:, BLK:, :], axis=0)
    pack = jnp.concatenate([along_z[:, :BLK, :].reshape(NZL * BLK, BLK), tail], axis=0)
    line = to_all(pack, AXES, 4, lines("yx"))
    cand = cand_blocks.T
    rings = lines("xy")
    swap = [(i, i ^ 1) for i in range(NX * NZH * NY * NZL * NC)]

    def swapped(value):
        return lax.ppermute(value, AXES, swap)

    cols = out_grad.shape[1] // BLK
    one, two, three = (lax.ppermute(line, AXES, shift(rings, by)) for by in (2, 1, 3))
    line_other = swapped(line)
    acc, turned = add_pieces(tokens, [line], cand, cols)
    one, acc = lax.optimization_barrier((one, acc))
    one_other = swapped(one)
    acc = add_pieces(tokens, [one, line_other], cand, cols, acc)
    two, three, acc = lax.optimization_barrier((two, three, acc))
    two_other, three_other = swapped(two), swapped(three)
    acc = add_pieces(tokens, [two, three, one_other], cand, cols, acc)
    acc, send = second_half(
        tokens, turned, [two_other, three_other], acc, out_grad, cand, group_counts
    )
    given = lax.ppermute(send, "c", [(0, 1), (1, 0)])
    keep = third_part(turned, acc, out_grad, cand, group_counts)
    mine = (keep.astype(jnp.float32) + given.astype(jnp.float32)).astype(jnp.bfloat16)
    mine = mine.reshape(NX * NY, NZL * (BLK // NX), BLK)
    planes = lax.all_to_all(mine, ("x", "y"), 0, 0, tiled=True)
    planes = planes.reshape(NX * NY, NZL, BLK // NX, BLK)
    strip = jnp.sum(planes.astype(jnp.float32), axis=0).astype(jnp.bfloat16)
    strips = jnp.broadcast_to(strip[None], (NZH,) + strip.shape).reshape(NZH * NZL, BLK // NX, BLK)
    strips = lax.all_to_all(strips, ("zh", "zl"), 0, 0, tiled=True)
    summed = jnp.sum(strips.astype(jnp.float32), axis=0)
    whole = to_all(summed, "x", NX).reshape(1, BLK, BLK)
    scale = (rows_dev * NX * NZH * NY * NZL * NC) ** (-0.5)
    cand_grad = whole * scale
    cand_score = jnp.sqrt(jnp.mean(cand_grad * cand_grad, axis=(1, 2)) + 1e-06)
    return (cand_grad, cand_score)


def solution(mesh):
    fine = Mesh(mesh.devices.reshape(SIZES), AXES)
    dp, fsdp = ("x", "zh"), ("y", "zl", "c")
    return jax.shard_map(
        per_device,
        mesh=fine,
        in_specs=(
            P(AXES, None),
            P(AXES, None),
            P(fsdp, None, None),
            P(fsdp, None),
            P(fsdp),
            P(),
            P(dp),
        ),
        out_specs=(P(fsdp, None, None), P(fsdp)),
        check_vma=False,
    )
```

```python
import functools

import jax
import jax.numpy as jnp
from jax import lax
from jax.experimental import pallas as pl
from jax.experimental.pallas import tpu as pltpu
from jax.sharding import Mesh, PartitionSpec as P

AXES = ("x", "zh", "y", "zl", "c")
SIZES = (4, 2, 4, 8, 2)
NX, NZH, NY, NZL, NC = SIZES
BLK = 128
TAIL = 16
PIECE = NZL * BLK + TAIL
MUL = 16
LIMIT1 = 20
LIMIT2 = 24


def flat(x, zh, y, zl, c):
    return (((x * NZH + zh) * NY + y) * NZL + zl) * NC + c


def runs_along_z():
    return [
        [flat(x, (z // NZL) % NZH, y, z % NZL, c) for z in range(start, start + NZL)]
        for c in range(NC)
        for x in range(NX)
        for y in range(NY)
        for start in (4 - 4 * c, 4 - 4 * c + NZL)
    ]


def shift(groups, by):
    return [(group[i], group[(i + by) % 4]) for group in groups for i in range(4)]


def lines(axis_of_core):
    groups = []
    for c, axis in enumerate(axis_of_core):
        for zh in range(NZH):
            for zl in range(NZL):
                for other in range(4):
                    if axis == "y":
                        groups.append([flat(other, zh, y, zl, c) for y in range(NY)])
                    else:
                        groups.append([flat(x, zh, other, zl, c) for x in range(NX)])
    return groups


def to_all(value, axis, count, groups=None):
    copies = jnp.broadcast_to(value[None], (count,) + value.shape)
    return lax.all_to_all(copies, axis, 0, 0, axis_index_groups=groups, tiled=True)


def gelu_slope(value_in):
    normal_cdf = 0.5 * (1.0 + lax.erf(value_in * 0.7071067811865476))
    density = jnp.exp(-0.5 * value_in * value_in) * 0.3989422804014327
    return normal_cdf + value_in * density


def read_places(tails, numbers, places, sem):
    row = lax.broadcasted_iota(jnp.int32, (TAIL, BLK), 0)
    for start in range(0, tails.shape[0], TAIL):
        table = jnp.zeros((TAIL, BLK), jnp.float32)
        for p in range(start, min(start + TAIL, tails.shape[0])):
            table = jnp.where(row == p - start, tails[p].astype(jnp.float32), table)
        numbers[pl.ds(start, TAIL), :] = table.astype(jnp.int32)
    move = pltpu.make_async_copy(numbers, places, sem)
    move.start()
    move.wait()


def choose_blocks(packs, places, slot_of, rows, slots, offs, spare, unroll):
    def choose(pack, count):
        found = [places[pack, 2 * z + 1] for z in range(NZL)]
        found = [slot_of[col] for col in found]
        where = [places[pack, 2 * z] for z in range(NZL)]
        for z in range(NZL):
            rows[count] = where[z]
            slots[count] = found[z]
            offs[count] = pack * NZL + z
            count = count + (found[z] != spare).astype(jnp.int32)
        return count

    count = lax.fori_loop(0, packs, choose, 0, unroll=2)
    for u in range(unroll):
        rows[count + u] = 0
        slots[count + u] = spare
        offs[count + u] = 0
    return count


def give_slots(cand, slot_of, spare):
    def clear(i, carry):
        slot_of[i] = spare
        return carry

    lax.fori_loop(0, slot_of.shape[0], clear, 0, unroll=8)

    def mark(j, count):
        col = cand[1, j]
        had = slot_of[col]
        fresh = had == spare
        slot_of[col] = jnp.where(fresh, count, had)
        return count + fresh.astype(jnp.int32)

    return lax.fori_loop(0, cand.shape[1], mark, 0, unroll=4)


def add_products(count, tok_ref, weights, acc, rows, slots, offs, unroll):
    def multiply(step, carry):
        products = []
        for u in range(unroll):
            i = step * unroll + u
            row = pl.multiple_of(rows[i] * BLK, BLK)
            pack = offs[i] // NZL
            off = pl.multiple_of(offs[i] % NZL * BLK, BLK)
            products.append(
                jnp.dot(
                    tok_ref[:, pl.ds(row, BLK)],
                    weights[pack, pl.ds(off, BLK), :],
                    preferred_element_type=jnp.float32,
                )
            )
        for u in range(unroll):
            acc[slots[step * unroll + u]] += products[u]
        return carry

    lax.fori_loop(0, (count + unroll - 1) // unroll, multiply, 0)


def piece_kernel(drop, active, blocks, out_ref, block, sem):
    slot = lax.axis_index("x")
    slot = slot + (slot >= drop[0]).astype(jnp.int32)
    fetch = pltpu.make_async_copy(blocks.at[slot], block, sem)
    fetch.start()
    lane = lax.broadcasted_iota(jnp.int32, (TAIL, BLK), 1)
    spot = 2 * ((lax.axis_index("zl") + 4 - 4 * lax.axis_index("c")) % NZL)
    tail = jnp.where(lane == spot, active[0, slot], 0)
    tail = jnp.where(lane == spot + 1, active[1, slot], tail)
    tail = tail.astype(jnp.float32).astype(jnp.bfloat16)
    for e in range(NZL):
        out_ref[e, pl.ds(BLK, TAIL), :] = tail
    fetch.wait()
    for e in range(NZL):
        out_ref[e, pl.ds(0, BLK), :] = block[...]


def first_pieces(drop, active, blocks):
    return pl.pallas_call(
        piece_kernel,
        out_shape=jax.ShapeDtypeStruct((NZL, BLK + TAIL, BLK), jnp.bfloat16),
        grid_spec=pltpu.PrefetchScalarGridSpec(
            num_scalar_prefetch=2,
            grid=(),
            in_specs=[ANY],
            out_specs=VMEM,
            scratch_shapes=[pltpu.VMEM((BLK, BLK), jnp.bfloat16), pltpu.SemaphoreType.DMA],
        ),
        compiler_params=pltpu.CompilerParams(vmem_limit_bytes=16 * 1024 * 1024),
    )(drop, active, blocks)


def fetch_pieces(pieces, weights, tails, sem, tail_sem):
    blocks, ends, at = [], [], 0
    for i, piece in enumerate(pieces):
        span = pl.ds(at, piece.shape[0])
        ends.append(
            pltpu.make_async_copy(
                piece.at[:, pl.ds(NZL * BLK, TAIL), :], tails.at[span], tail_sem.at[i]
            )
        )
        blocks.append(pltpu.make_async_copy(piece, weights.at[span], sem.at[i]))
        at += piece.shape[0]
    for copy in ends + blocks:
        copy.start()

    def wait(copies):
        for copy in copies:
            copy.wait()

    return functools.partial(wait, ends), functools.partial(wait, blocks)


def add_kernel(count, later, cand, tok_ref, *refs):
    pieces, refs = refs[:count], refs[count:]
    if later:
        (before, acc), refs = refs[:2], refs[2:]
    else:
        (acc, turned), refs = refs[:2], refs[2:]
    (weights, tails, numbers, places, slot_of, rows, slots, offs,
     sem, tail_sem, move_sem) = refs
    wait_tails, wait_blocks = fetch_pieces(pieces, weights, tails, sem, tail_sem)
    spare = acc.shape[0] - 1
    give_slots(cand, slot_of, spare)

    def begin(i, carry):
        acc[i] = before[i] if later else jnp.zeros(acc.shape[1:], jnp.float32)
        return carry

    lax.fori_loop(0, spare + 1, begin, 0, unroll=5)
    wait_tails()
    read_places(tails, numbers, places, move_sem)
    found = choose_blocks(tails.shape[0], places, slot_of, rows, slots, offs, spare, MUL)
    if not later:
        for r in range(turned.shape[0]):
            turned[r] = tok_ref[:, r * BLK : (r + 1) * BLK].T
    wait_blocks()
    add_products(found, tok_ref, weights, acc, rows, slots, offs, MUL)


def gradients(core, cand, counts, turned, slot_of, acc, grad_ref, out_ref):
    tokens = acc.shape[1]
    index = (lax.axis_index("y") * NZL + lax.axis_index("zl")) * NC + lax.axis_index("c")
    position = index * tokens + lax.broadcasted_iota(jnp.int32, (tokens, BLK), 0)
    usable = (position < counts[0]).astype(jnp.float32)

    def gradient(q, carry):
        y, z = q // NZL, q % NZL
        j = q * NC + core
        col = cand[1, j]
        lanes = pl.ds(pl.multiple_of(col * BLK, BLK), BLK)
        slope = gelu_slope(acc[slot_of[col]])
        given = grad_ref[:, lanes].astype(jnp.float32)
        part = jnp.dot(
            turned[cand[0, j]],
            (given * slope * usable).astype(jnp.bfloat16),
            preferred_element_type=jnp.float32,
        ).astype(jnp.bfloat16)
        for x in range(NX):
            out_ref[x, y, z] = part[x * 32 : (x + 1) * 32]
        return carry

    lax.fori_loop(0, cand.shape[1] // NC, gradient, 0, unroll=16)


def second_kernel(
    cand, counts, tok_ref, turned, one, two, three, four, before, grad_ref, acc, send_ref,
    weights, tails, numbers, places, slot_of, rows, slots, offs, sem, tail_sem, move_sem,
):
    wait_tails, wait_blocks = fetch_pieces([one, two, three, four], weights, tails, sem, tail_sem)
    spare = acc.shape[0] - 1
    give_slots(cand, slot_of, spare)

    def begin(i, carry):
        acc[i] = before[i]
        return carry

    lax.fori_loop(0, spare + 1, begin, 0, unroll=5)
    wait_tails()
    read_places(tails, numbers, places, move_sem)
    found = choose_blocks(tails.shape[0], places, slot_of, rows, slots, offs, spare, MUL)
    wait_blocks()
    add_products(found, tok_ref, weights, acc, rows, slots, offs, MUL)
    gradients(
        1 - lax.axis_index("c"), cand, counts, turned, slot_of, acc, grad_ref, send_ref
    )


def third_kernel(cand, counts, turned, acc, grad_ref, keep_ref, slot_of):
    give_slots(cand, slot_of, acc.shape[0] - 1)
    gradients(lax.axis_index("c"), cand, counts, turned, slot_of, acc, grad_ref, keep_ref)


def place_scratch(packs):
    return [
        pltpu.VMEM((packs, TAIL, BLK), jnp.bfloat16),
        pltpu.VMEM((pl.cdiv(packs, TAIL) * TAIL, BLK), jnp.int32),
        pltpu.SMEM((pl.cdiv(packs, TAIL) * TAIL, BLK), jnp.int32),
    ]


def lists(cols, stored):
    smem = lambda count: pltpu.SMEM((count,), jnp.int32)
    return [smem(cols)] + [smem(stored + 2 * MUL)] * 3


VMEM = pl.BlockSpec(memory_space=pltpu.VMEM)
ANY = pl.BlockSpec(memory_space=pl.ANY)


def add_pieces(tokens, pieces, cand, col_blocks, before=None):
    packs, cands = sum(piece.shape[0] for piece in pieces), cand.shape[1]
    rows_dev, count = tokens.shape[0], len(pieces)
    later = before is not None
    sums = jax.ShapeDtypeStruct((cands + 1, rows_dev, BLK), jnp.float32)
    turned = jax.ShapeDtypeStruct((tokens.shape[1] // BLK, BLK, rows_dev), jnp.bfloat16)
    return pl.pallas_call(
        functools.partial(add_kernel, count, later),
        out_shape=sums if later else (sums, turned),
        grid_spec=pltpu.PrefetchScalarGridSpec(
            num_scalar_prefetch=1,
            grid=(),
            in_specs=[VMEM] + [ANY] * count + [VMEM] * later,
            out_specs=VMEM if later else (VMEM, VMEM),
            scratch_shapes=[pltpu.VMEM((packs, PIECE, BLK), jnp.bfloat16)]
            + place_scratch(packs)
            + lists(col_blocks, packs * NZL)
            + [pltpu.SemaphoreType.DMA((count,))] * 2
            + [pltpu.SemaphoreType.DMA],
        ),
        compiler_params=pltpu.CompilerParams(vmem_limit_bytes=LIMIT1 * 1024 * 1024),
        cost_estimate=pl.CostEstimate(
            flops=2 * packs * NZL * rows_dev * BLK * BLK,
            bytes_accessed=10_000_000,
            transcendentals=0,
        ),
    )(cand, tokens, *pieces, *([before] if later else []))


PART = jax.ShapeDtypeStruct((NX, NY, NZL, BLK // NX, BLK), jnp.bfloat16)


def second_half(tokens, turned, pieces, before, out_grad, cand, counts):
    packs = sum(piece.shape[0] for piece in pieces)
    col_blocks = out_grad.shape[1] // BLK
    rows_dev = tokens.shape[0]
    return pl.pallas_call(
        second_kernel,
        out_shape=(jax.ShapeDtypeStruct(before.shape, jnp.float32), PART),
        grid_spec=pltpu.PrefetchScalarGridSpec(
            num_scalar_prefetch=2,
            grid=(),
            in_specs=[VMEM, VMEM] + [ANY] * len(pieces) + [VMEM, VMEM],
            out_specs=(VMEM, VMEM),
            scratch_shapes=[pltpu.VMEM((packs, PIECE, BLK), jnp.bfloat16)]
            + place_scratch(packs)
            + lists(col_blocks, packs * NZL)
            + [pltpu.SemaphoreType.DMA((len(pieces),))] * 2
            + [pltpu.SemaphoreType.DMA],
        ),
        compiler_params=pltpu.CompilerParams(vmem_limit_bytes=LIMIT2 * 1024 * 1024),
        cost_estimate=pl.CostEstimate(
            flops=2 * (packs * NZL + 32) * rows_dev * BLK * BLK,
            bytes_accessed=15_000_000,
            transcendentals=1_000_000,
        ),
    )(cand, counts, tokens, turned, *pieces, before, out_grad)


def third_part(turned, acc, out_grad, cand, counts):
    return pl.pallas_call(
        third_kernel,
        out_shape=PART,
        grid_spec=pltpu.PrefetchScalarGridSpec(
            num_scalar_prefetch=2,
            grid=(),
            in_specs=[VMEM, VMEM, VMEM],
            out_specs=VMEM,
            scratch_shapes=[pltpu.SMEM((out_grad.shape[1] // BLK,), jnp.int32)],
        ),
        compiler_params=pltpu.CompilerParams(vmem_limit_bytes=LIMIT2 * 1024 * 1024),
        cost_estimate=pl.CostEstimate(
            flops=2 * 32 * BLK**3, bytes_accessed=8_000_000, transcendentals=1_000_000
        ),
    )(cand, counts, turned, acc, out_grad)


def per_device(
    tokens, out_grad, block_values, active_blocks, drop_slots, cand_blocks, group_counts
):
    rows_dev = tokens.shape[0]
    pieces = first_pieces(drop_slots, active_blocks.T, block_values)
    along_z = lax.all_to_all(
        pieces, AXES, 0, 0, axis_index_groups=runs_along_z(), tiled=True
    )
    tail = jnp.sum(along_z[:, BLK:, :], axis=0)
    pack = jnp.concatenate([along_z[:, :BLK, :].reshape(NZL * BLK, BLK), tail], axis=0)
    line = to_all(pack, AXES, 4, lines("yx"))
    cand = cand_blocks.T
    rings = lines("xy")
    swap = [(i, i ^ 1) for i in range(NX * NZH * NY * NZL * NC)]

    def swapped(value):
        return lax.ppermute(value, AXES, swap)

    cols = out_grad.shape[1] // BLK
    one, two, three = (lax.ppermute(line, AXES, shift(rings, by)) for by in (2, 1, 3))
    line_other = swapped(line)
    acc, turned = add_pieces(tokens, [line], cand, cols)
    one, acc = lax.optimization_barrier((one, acc))
    one_other = swapped(one)
    acc = add_pieces(tokens, [one, line_other], cand, cols, acc)
    two, three, one_other, acc = lax.optimization_barrier((two, three, one_other, acc))
    both_other = swapped(jnp.concatenate([two, three], axis=0))
    acc, send = second_half(
        tokens,
        turned,
        [two, three, one_other, both_other],
        acc,
        out_grad,
        cand,
        group_counts,
    )
    given = lax.ppermute(send, "c", [(0, 1), (1, 0)])
    keep = third_part(turned, acc, out_grad, cand, group_counts)
    mine = (keep.astype(jnp.float32) + given.astype(jnp.float32)).astype(jnp.bfloat16)
    mine = mine.reshape(NX * NY, NZL * (BLK // NX), BLK)
    planes = lax.all_to_all(mine, ("x", "y"), 0, 0, tiled=True)
    planes = planes.reshape(NX * NY, NZL, BLK // NX, BLK)
    strip = jnp.sum(planes.astype(jnp.float32), axis=0).astype(jnp.bfloat16)
    strips = jnp.broadcast_to(strip[None], (NZH,) + strip.shape).reshape(NZH * NZL, BLK // NX, BLK)
    strips = lax.all_to_all(strips, ("zh", "zl"), 0, 0, tiled=True)
    summed = jnp.sum(strips.astype(jnp.float32), axis=0)
    whole = to_all(summed, "x", NX).reshape(1, BLK, BLK)
    scale = (rows_dev * NX * NZH * NY * NZL * NC) ** (-0.5)
    cand_grad = whole * scale
    cand_score = jnp.sqrt(jnp.mean(cand_grad * cand_grad, axis=(1, 2)) + 1e-06)
    return (cand_grad, cand_score)


def solution(mesh):
    fine = Mesh(mesh.devices.reshape(SIZES), AXES)
    dp, fsdp = ("x", "zh"), ("y", "zl", "c")
    return jax.shard_map(
        per_device,
        mesh=fine,
        in_specs=(
            P(AXES, None),
            P(AXES, None),
            P(fsdp, None, None),
            P(fsdp, None),
            P(fsdp),
            P(),
            P(dp),
        ),
        out_specs=(P(fsdp, None, None), P(fsdp)),
        check_vma=False,
    )
```

```python
import functools

import jax
import jax.numpy as jnp
from jax import lax
from jax.experimental import pallas as pl
from jax.experimental.pallas import tpu as pltpu
from jax.sharding import Mesh, PartitionSpec as P

AXES = ("x", "zh", "y", "zl", "c")
SIZES = (4, 2, 4, 8, 2)
NX, NZH, NY, NZL, NC = SIZES
BLK = 128
TAIL = 16
PIECE = NZL * BLK + TAIL
MUL = 16
LIMIT1 = 20
LIMIT2 = 24


def flat(x, zh, y, zl, c):
    return (((x * NZH + zh) * NY + y) * NZL + zl) * NC + c


def runs_along_z():
    return [
        [flat(x, (z // NZL) % NZH, y, z % NZL, c) for z in range(start, start + NZL)]
        for c in range(NC)
        for x in range(NX)
        for y in range(NY)
        for start in (4 - 4 * c, 4 - 4 * c + NZL)
    ]


def shift(groups, by):
    return [(group[i], group[(i + by) % 4]) for group in groups for i in range(4)]


def lines(axis_of_core):
    groups = []
    for c, axis in enumerate(axis_of_core):
        for zh in range(NZH):
            for zl in range(NZL):
                for other in range(4):
                    if axis == "y":
                        groups.append([flat(other, zh, y, zl, c) for y in range(NY)])
                    else:
                        groups.append([flat(x, zh, other, zl, c) for x in range(NX)])
    return groups


def to_all(value, axis, count, groups=None):
    copies = jnp.broadcast_to(value[None], (count,) + value.shape)
    return lax.all_to_all(copies, axis, 0, 0, axis_index_groups=groups, tiled=True)


def gelu_slope(value_in):
    normal_cdf = 0.5 * (1.0 + lax.erf(value_in * 0.7071067811865476))
    density = jnp.exp(-0.5 * value_in * value_in) * 0.3989422804014327
    return normal_cdf + value_in * density


def read_places(tails, numbers, places, sem):
    row = lax.broadcasted_iota(jnp.int32, (TAIL, BLK), 0)
    for start in range(0, tails.shape[0], TAIL):
        table = jnp.zeros((TAIL, BLK), jnp.float32)
        for p in range(start, min(start + TAIL, tails.shape[0])):
            table = jnp.where(row == p - start, tails[p].astype(jnp.float32), table)
        numbers[pl.ds(start, TAIL), :] = table.astype(jnp.int32)
    move = pltpu.make_async_copy(numbers, places, sem)
    move.start()
    move.wait()


def choose_blocks(packs, places, slot_of, rows, slots, offs, spare, unroll):
    def choose(pack, count):
        found = [places[pack, 2 * z + 1] for z in range(NZL)]
        found = [slot_of[col] for col in found]
        where = [places[pack, 2 * z] for z in range(NZL)]
        for z in range(NZL):
            rows[count] = where[z]
            slots[count] = found[z]
            offs[count] = pack * NZL + z
            count = count + (found[z] != spare).astype(jnp.int32)
        return count

    count = lax.fori_loop(0, packs, choose, 0, unroll=2)
    for u in range(unroll):
        rows[count + u] = 0
        slots[count + u] = spare
        offs[count + u] = 0
    return count


def give_slots(cand, slot_of, spare):
    def clear(i, carry):
        slot_of[i] = spare
        return carry

    lax.fori_loop(0, slot_of.shape[0], clear, 0, unroll=8)

    def mark(j, count):
        col = cand[1, j]
        had = slot_of[col]
        fresh = had == spare
        slot_of[col] = jnp.where(fresh, count, had)
        return count + fresh.astype(jnp.int32)

    return lax.fori_loop(0, cand.shape[1], mark, 0, unroll=4)


def add_products(count, tok_ref, weights, acc, rows, slots, offs, unroll):
    def multiply(step, carry):
        products = []
        for u in range(unroll):
            i = step * unroll + u
            row = pl.multiple_of(rows[i] * BLK, BLK)
            pack = offs[i] // NZL
            off = pl.multiple_of(offs[i] % NZL * BLK, BLK)
            products.append(
                jnp.dot(
                    tok_ref[:, pl.ds(row, BLK)],
                    weights[pack, pl.ds(off, BLK), :],
                    preferred_element_type=jnp.float32,
                )
            )
        for u in range(unroll):
            acc[slots[step * unroll + u]] += products[u]
        return carry

    lax.fori_loop(0, (count + unroll - 1) // unroll, multiply, 0)


def piece_kernel(drop, active, blocks, out_ref, block, sem):
    slot = lax.axis_index("x")
    slot = slot + (slot >= drop[0]).astype(jnp.int32)
    fetch = pltpu.make_async_copy(blocks.at[slot], block, sem)
    fetch.start()
    lane = lax.broadcasted_iota(jnp.int32, (TAIL, BLK), 1)
    spot = 2 * ((lax.axis_index("zl") + 4 - 4 * lax.axis_index("c")) % NZL)
    tail = jnp.where(lane == spot, active[0, slot], 0)
    tail = jnp.where(lane == spot + 1, active[1, slot], tail)
    tail = tail.astype(jnp.float32).astype(jnp.bfloat16)
    for e in range(NZL):
        out_ref[e, pl.ds(BLK, TAIL), :] = tail
    fetch.wait()
    for e in range(NZL):
        out_ref[e, pl.ds(0, BLK), :] = block[...]


def first_pieces(drop, active, blocks):
    return pl.pallas_call(
        piece_kernel,
        out_shape=jax.ShapeDtypeStruct((NZL, BLK + TAIL, BLK), jnp.bfloat16),
        grid_spec=pltpu.PrefetchScalarGridSpec(
            num_scalar_prefetch=2,
            grid=(),
            in_specs=[ANY],
            out_specs=VMEM,
            scratch_shapes=[pltpu.VMEM((BLK, BLK), jnp.bfloat16), pltpu.SemaphoreType.DMA],
        ),
        compiler_params=pltpu.CompilerParams(vmem_limit_bytes=16 * 1024 * 1024),
    )(drop, active, blocks)


def fetch_pieces(pieces, weights, tails, sem, tail_sem):
    blocks, ends, at = [], [], 0
    for i, piece in enumerate(pieces):
        span = pl.ds(at, piece.shape[0])
        ends.append(
            pltpu.make_async_copy(
                piece.at[:, pl.ds(NZL * BLK, TAIL), :], tails.at[span], tail_sem.at[i]
            )
        )
        blocks.append(pltpu.make_async_copy(piece, weights.at[span], sem.at[i]))
        at += piece.shape[0]
    for copy in ends + blocks:
        copy.start()

    def wait(copies):
        for copy in copies:
            copy.wait()

    return functools.partial(wait, ends), functools.partial(wait, blocks)


def add_kernel(count, later, cand, tok_ref, *refs):
    pieces, refs = refs[:count], refs[count:]
    if later:
        (before, acc), refs = refs[:2], refs[2:]
    else:
        (acc, turned), refs = refs[:2], refs[2:]
    (weights, tails, numbers, places, slot_of, rows, slots, offs,
     sem, tail_sem, move_sem) = refs
    wait_tails, wait_blocks = fetch_pieces(pieces, weights, tails, sem, tail_sem)
    spare = acc.shape[0] - 1
    give_slots(cand, slot_of, spare)

    def begin(i, carry):
        acc[i] = before[i] if later else jnp.zeros(acc.shape[1:], jnp.float32)
        return carry

    lax.fori_loop(0, spare + 1, begin, 0, unroll=5)
    wait_tails()
    read_places(tails, numbers, places, move_sem)
    found = choose_blocks(tails.shape[0], places, slot_of, rows, slots, offs, spare, MUL)
    if not later:
        for r in range(turned.shape[0]):
            turned[r] = tok_ref[:, r * BLK : (r + 1) * BLK].T
    wait_blocks()
    add_products(found, tok_ref, weights, acc, rows, slots, offs, MUL)


def gradients(core, cand, counts, turned, slot_of, acc, grad_ref, out_ref):
    tokens = acc.shape[1]
    index = (lax.axis_index("y") * NZL + lax.axis_index("zl")) * NC + lax.axis_index("c")
    position = index * tokens + lax.broadcasted_iota(jnp.int32, (tokens, BLK), 0)
    usable = (position < counts[0]).astype(jnp.float32)

    def gradient(q, carry):
        y, z = q // NZL, q % NZL
        j = q * NC + core
        col = cand[1, j]
        lanes = pl.ds(pl.multiple_of(col * BLK, BLK), BLK)
        slope = gelu_slope(acc[slot_of[col]])
        given = grad_ref[:, lanes].astype(jnp.float32)
        part = jnp.dot(
            turned[cand[0, j]],
            (given * slope * usable).astype(jnp.bfloat16),
            preferred_element_type=jnp.float32,
        ).astype(jnp.bfloat16)
        for x in range(NX):
            out_ref[x, y, z] = part[x * 32 : (x + 1) * 32]
        return carry

    lax.fori_loop(0, cand.shape[1] // NC, gradient, 0, unroll=32)


def second_kernel(
    cand, counts, tok_ref, turned, one, two, before, grad_ref, acc, send_ref,
    weights, tails, numbers, places, slot_of, rows, slots, offs, sem, tail_sem, move_sem,
):
    wait_tails, wait_blocks = fetch_pieces([one, two], weights, tails, sem, tail_sem)
    spare = acc.shape[0] - 1
    give_slots(cand, slot_of, spare)

    def begin(i, carry):
        acc[i] = before[i]
        return carry

    lax.fori_loop(0, spare + 1, begin, 0, unroll=5)
    wait_tails()
    read_places(tails, numbers, places, move_sem)
    found = choose_blocks(tails.shape[0], places, slot_of, rows, slots, offs, spare, MUL)
    wait_blocks()
    add_products(found, tok_ref, weights, acc, rows, slots, offs, MUL)
    gradients(
        1 - lax.axis_index("c"), cand, counts, turned, slot_of, acc, grad_ref, send_ref
    )


def third_kernel(cand, counts, turned, acc, grad_ref, keep_ref, slot_of):
    give_slots(cand, slot_of, acc.shape[0] - 1)
    gradients(lax.axis_index("c"), cand, counts, turned, slot_of, acc, grad_ref, keep_ref)


def place_scratch(packs):
    return [
        pltpu.VMEM((packs, TAIL, BLK), jnp.bfloat16),
        pltpu.VMEM((pl.cdiv(packs, TAIL) * TAIL, BLK), jnp.int32),
        pltpu.SMEM((pl.cdiv(packs, TAIL) * TAIL, BLK), jnp.int32),
    ]


def lists(cols, stored):
    smem = lambda count: pltpu.SMEM((count,), jnp.int32)
    return [smem(cols)] + [smem(stored + 2 * MUL)] * 3


VMEM = pl.BlockSpec(memory_space=pltpu.VMEM)
ANY = pl.BlockSpec(memory_space=pl.ANY)


def add_pieces(tokens, pieces, cand, col_blocks, before=None):
    packs, cands = sum(piece.shape[0] for piece in pieces), cand.shape[1]
    rows_dev, count = tokens.shape[0], len(pieces)
    later = before is not None
    sums = jax.ShapeDtypeStruct((cands + 1, rows_dev, BLK), jnp.float32)
    turned = jax.ShapeDtypeStruct((tokens.shape[1] // BLK, BLK, rows_dev), jnp.bfloat16)
    return pl.pallas_call(
        functools.partial(add_kernel, count, later),
        out_shape=sums if later else (sums, turned),
        grid_spec=pltpu.PrefetchScalarGridSpec(
            num_scalar_prefetch=1,
            grid=(),
            in_specs=[VMEM] + [ANY] * count + [VMEM] * later,
            out_specs=VMEM if later else (VMEM, VMEM),
            scratch_shapes=[pltpu.VMEM((packs, PIECE, BLK), jnp.bfloat16)]
            + place_scratch(packs)
            + lists(col_blocks, packs * NZL)
            + [pltpu.SemaphoreType.DMA((count,))] * 2
            + [pltpu.SemaphoreType.DMA],
        ),
        compiler_params=pltpu.CompilerParams(vmem_limit_bytes=LIMIT1 * 1024 * 1024),
        cost_estimate=pl.CostEstimate(
            flops=2 * packs * NZL * rows_dev * BLK * BLK,
            bytes_accessed=10_000_000,
            transcendentals=0,
        ),
    )(cand, tokens, *pieces, *([before] if later else []))


PART = jax.ShapeDtypeStruct((NX, NY, NZL, BLK // NX, BLK), jnp.bfloat16)


def second_half(tokens, turned, pieces, before, out_grad, cand, counts):
    packs = sum(piece.shape[0] for piece in pieces)
    col_blocks = out_grad.shape[1] // BLK
    rows_dev = tokens.shape[0]
    return pl.pallas_call(
        second_kernel,
        out_shape=(jax.ShapeDtypeStruct(before.shape, jnp.float32), PART),
        grid_spec=pltpu.PrefetchScalarGridSpec(
            num_scalar_prefetch=2,
            grid=(),
            in_specs=[VMEM, VMEM] + [ANY] * len(pieces) + [VMEM, VMEM],
            out_specs=(VMEM, VMEM),
            scratch_shapes=[pltpu.VMEM((packs, PIECE, BLK), jnp.bfloat16)]
            + place_scratch(packs)
            + lists(col_blocks, packs * NZL)
            + [pltpu.SemaphoreType.DMA((len(pieces),))] * 2
            + [pltpu.SemaphoreType.DMA],
        ),
        compiler_params=pltpu.CompilerParams(vmem_limit_bytes=LIMIT2 * 1024 * 1024),
        cost_estimate=pl.CostEstimate(
            flops=2 * (packs * NZL + 32) * rows_dev * BLK * BLK,
            bytes_accessed=15_000_000,
            transcendentals=1_000_000,
        ),
    )(cand, counts, tokens, turned, *pieces, before, out_grad)


def third_part(turned, acc, out_grad, cand, counts):
    return pl.pallas_call(
        third_kernel,
        out_shape=PART,
        grid_spec=pltpu.PrefetchScalarGridSpec(
            num_scalar_prefetch=2,
            grid=(),
            in_specs=[VMEM, VMEM, VMEM],
            out_specs=VMEM,
            scratch_shapes=[pltpu.SMEM((out_grad.shape[1] // BLK,), jnp.int32)],
        ),
        compiler_params=pltpu.CompilerParams(vmem_limit_bytes=LIMIT2 * 1024 * 1024),
        cost_estimate=pl.CostEstimate(
            flops=2 * 32 * BLK**3, bytes_accessed=8_000_000, transcendentals=1_000_000
        ),
    )(cand, counts, turned, acc, out_grad)


def per_device(
    tokens, out_grad, block_values, active_blocks, drop_slots, cand_blocks, group_counts
):
    rows_dev = tokens.shape[0]
    pieces = first_pieces(drop_slots, active_blocks.T, block_values)
    along_z = lax.all_to_all(
        pieces, AXES, 0, 0, axis_index_groups=runs_along_z(), tiled=True
    )
    tail = jnp.sum(along_z[:, BLK:, :], axis=0)
    pack = jnp.concatenate([along_z[:, :BLK, :].reshape(NZL * BLK, BLK), tail], axis=0)
    line = to_all(pack, AXES, 4, lines("yx"))
    cand = cand_blocks.T
    rings = lines("xy")
    swap = [(i, i ^ 1) for i in range(NX * NZH * NY * NZL * NC)]

    def swapped(value):
        return lax.ppermute(value, AXES, swap)

    cols = out_grad.shape[1] // BLK
    one, two, three = (lax.ppermute(line, AXES, shift(rings, by)) for by in (2, 1, 3))
    line_other = swapped(line)
    acc, turned = add_pieces(tokens, [line], cand, cols)
    one, acc = lax.optimization_barrier((one, acc))
    one_other = swapped(one)
    acc = add_pieces(tokens, [one, line_other], cand, cols, acc)
    two, three, one_other, acc = lax.optimization_barrier((two, three, one_other, acc))
    both_other = swapped(jnp.concatenate([two, three], axis=0))
    acc = add_pieces(tokens, [two, three], cand, cols, acc)
    acc, send = second_half(
        tokens, turned, [one_other, both_other], acc, out_grad, cand, group_counts
    )
    given = lax.ppermute(send, "c", [(0, 1), (1, 0)])
    keep = third_part(turned, acc, out_grad, cand, group_counts)
    mine = (keep.astype(jnp.float32) + given.astype(jnp.float32)).astype(jnp.bfloat16)
    mine = mine.reshape(NX * NY, NZL * (BLK // NX), BLK)
    planes = lax.all_to_all(mine, ("x", "y"), 0, 0, tiled=True)
    planes = planes.reshape(NX * NY, NZL, BLK // NX, BLK)
    strip = jnp.sum(planes.astype(jnp.float32), axis=0).astype(jnp.bfloat16)
    strips = jnp.broadcast_to(strip[None], (NZH,) + strip.shape).reshape(NZH * NZL, BLK // NX, BLK)
    strips = lax.all_to_all(strips, ("zh", "zl"), 0, 0, tiled=True)
    summed = jnp.sum(strips.astype(jnp.float32), axis=0)
    whole = to_all(summed, "x", NX).reshape(1, BLK, BLK)
    scale = (rows_dev * NX * NZH * NY * NZL * NC) ** (-0.5)
    cand_grad = whole * scale
    cand_score = jnp.sqrt(jnp.mean(cand_grad * cand_grad, axis=(1, 2)) + 1e-06)
    return (cand_grad, cand_score)


def solution(mesh):
    fine = Mesh(mesh.devices.reshape(SIZES), AXES)
    dp, fsdp = ("x", "zh"), ("y", "zl", "c")
    return jax.shard_map(
        per_device,
        mesh=fine,
        in_specs=(
            P(AXES, None),
            P(AXES, None),
            P(fsdp, None, None),
            P(fsdp, None),
            P(fsdp),
            P(),
            P(dp),
        ),
        out_specs=(P(fsdp, None, None), P(fsdp)),
        check_vma=False,
    )
```
